768 devices in a mesh: node: 32 (over x, y), local: 24 (over z, core).
Axes of the slice: x: 4, y: 8, z: 12, core: 2. Of those that a mesh axis runs over, the one named last changes fastest.
Arguments:
- grads: bfloat16 [98304, 5376], P(('node', 'local')), may hold values from -6 to 6
- token_slot: int32 [98304], P(('node', 'local')), may hold values from 0 to 383, as said below
- node_ids: int32 [32, 384], P('node', 'local'), may hold values from 0 to 262135, as said below
- touched_ids: int32 [12288], P(('node', 'local')), may hold values from -1 to 262135, as said below
- owner_map: int32 [768, 32, 2], P(('node', 'local')), may hold values from -1 to 15, as said below
- moment: float32 [12288, 5376], P(('node', 'local')), may hold values from -4 to 4
- second: float32 [12288, 5376], P(('node', 'local')), may hold values from 0.01 to 1
- master: float32 [12288, 5376], P(('node', 'local')), may hold values from -0.12 to 0.12
Outputs:
- token_rows: bfloat16 [98304, 5376], P(('node', 'local'))
- moment_out: float32 [12288, 5376], P(('node', 'local'))
- second_out: float32 [12288, 5376], P(('node', 'local'))
- master_out: float32 [12288, 5376], P(('node', 'local'))
The draws below stay inside these ranges and needn't reach their ends.
Inputs may be any that keep to these rules, and one draw needn't show every extreme that they name: `node_ids`: within one device's 16 entries the ids are distinct and at most 2 of them share an owner node id // 8192; for each local index one owner node receives exactly 2 ids from every node's device of that local index. `token_slot`: every entry of a node's list is used by some token of that node. `touched_ids`: on device (o, j) the entries that are not -1 are distinct ids with owner node o, and they are exactly the ids that devices of local index j list with owner node o. `owner_map`: on device (o, j), entry [n, c] is the position in this device's touched_ids of the c-th id, in list order, that device (n, j) lists with owner node o, and -1 where device (n, j) lists fewer than c + 1 such ids.
All inputs are finite; a program needn't handle non-finite values.
Results may differ from the reference program's by a relative error of at most 0.014.
Values may be sent and summed in bfloat16 or wider, within the bound.
No kernel may reach another device: no remote copies, remote signals or barrier semaphores. Data moves between devices by JAX's collectives and lax.ppermute only.
A program may use at most 32 MiB of HBM per device.

```python
import math
import jax
import jax.numpy as jnp
from jax import lax

D = 5376
VOCAB = 262144
TOK_DEV = 128
SLOT_DEV = 16
CAP = 2
TOUCH_CAP = 16
STEP = 100
TOKENS = 98304
TOUCHED = 12288
N_NODE = 32
N_LOCAL = 24


def layout(key):
    subkeys = jax.random.split(key, 8)
    dest_slots = N_NODE * CAP
    rows_node = VOCAB // N_NODE
    reach = rows_node // N_LOCAL
    local_range = jnp.arange(N_LOCAL, dtype=jnp.int32)
    crowded = jnp.where(local_range == N_LOCAL - 1, N_NODE - 1, jax.random.randint(subkeys[0], (N_LOCAL,), 0, N_NODE))
    slot_owner = jnp.arange(dest_slots, dtype=jnp.int32) // CAP
    preference = (slot_owner[None, None, :] == crowded[None, :, None]).astype(jnp.int32) * (1 << 29)
    scores = jax.random.randint(subkeys[1], (N_NODE, N_LOCAL, dest_slots), 0, 1 << 20) * dest_slots + jnp.arange(dest_slots, dtype=jnp.int32)
    chosen = lax.top_k(scores + preference, SLOT_DEV)[1]
    mixing = jax.random.randint(subkeys[2], (N_NODE, N_LOCAL, SLOT_DEV), 0, 1 << 20) * SLOT_DEV + jnp.arange(SLOT_DEV, dtype=jnp.int32)
    shuffled = lax.top_k(mixing, SLOT_DEV)[1]
    target = jnp.take_along_axis(chosen, shuffled, axis=2) // CAP
    same_owner = target[:, :, :, None] == target[:, :, None, :]
    positions = jnp.arange(SLOT_DEV, dtype=jnp.int32)
    earlier = positions[None, :] < positions[:, None]
    rank_slot = jnp.sum((same_owner & earlier[None, None]).astype(jnp.int32), axis=3)
    first_pos = jnp.minimum(jax.random.randint(subkeys[3], (N_NODE, N_LOCAL, N_NODE), 0, TOUCH_CAP), jax.random.randint(subkeys[4], (N_NODE, N_LOCAL, N_NODE), 0, TOUCH_CAP))
    stride = 1 + jax.random.randint(subkeys[5], (N_NODE, N_LOCAL, N_NODE), 0, TOUCH_CAP - 1)
    shift_pos = jax.random.randint(subkeys[6], (N_LOCAL,), 0, TOUCH_CAP)
    spread_pos = (jnp.take_along_axis(first_pos, target, axis=2) + rank_slot * jnp.take_along_axis(stride, target, axis=2)) % TOUCH_CAP
    node_index = jnp.arange(N_NODE, dtype=jnp.int32)[:, None, None]
    local_index = local_range[None, :, None]
    packed_pos = (node_index * CAP + rank_slot + shift_pos[None, :, None]) % TOUCH_CAP
    position = jnp.where(target == crowded[None, :, None], packed_pos, spread_pos)
    owner_device = target * N_LOCAL + local_index
    flat_map = (owner_device * N_NODE + node_index) * CAP + rank_slot
    owner_map = jnp.full((N_NODE * N_LOCAL * N_NODE * CAP,), -1, jnp.int32).at[flat_map.reshape(-1)].set(position.reshape(-1))
    touched_flat = (owner_device * TOUCH_CAP + position).reshape(-1)
    occupied = jnp.zeros((N_NODE * N_LOCAL * TOUCH_CAP,), jnp.int32).at[touched_flat].max(1)
    reach_index = jnp.arange(reach, dtype=jnp.int32)[None, :]
    row_scores = jax.random.randint(subkeys[7], (N_NODE * N_LOCAL, reach), 0, 1 << 14) * reach + reach_index
    row_scores = row_scores + (reach_index == reach - 1).astype(jnp.int32) * (1 << 30)
    picks = lax.top_k(row_scores, TOUCH_CAP)[1]
    touch_index = jnp.arange(TOUCH_CAP, dtype=jnp.int32)[None, :]
    occupied_rows = occupied.reshape(N_NODE * N_LOCAL, TOUCH_CAP)
    first_occ = jnp.min(jnp.where(occupied_rows > 0, touch_index, TOUCH_CAP), axis=1) % TOUCH_CAP
    pick_order = (touch_index - first_occ[:, None]) % TOUCH_CAP
    placed_picks = jnp.take_along_axis(picks, pick_order, axis=1)
    device_index = jnp.arange(N_NODE * N_LOCAL, dtype=jnp.int32)
    owner_ids = (device_index // N_LOCAL)[:, None] * rows_node + (device_index % N_LOCAL)[:, None] + N_LOCAL * placed_picks
    owner_ids = owner_ids.reshape(-1).astype(jnp.int32)
    touched = jnp.where(occupied > 0, owner_ids, -1).astype(jnp.int32)
    node_ids = owner_ids[touched_flat].reshape(N_NODE, N_LOCAL * SLOT_DEV)
    return (node_ids, touched, owner_map.reshape(N_NODE * N_LOCAL, N_NODE, CAP))


def draw_node_ids(key, part):
    listed, touched, mapping = layout(key)
    return listed


def draw_touched_ids(key, part):
    listed, touched, mapping = layout(key)
    return touched


def draw_owner_map(key, part):
    listed, touched, mapping = layout(key)
    return mapping


def draw_token_slot(key, part):
    key = jax.random.fold_in(key, 11)
    list_len = N_LOCAL * SLOT_DEV
    node_tokens = N_LOCAL * TOK_DEV
    key_one, key_two, key_three, key_four = jax.random.split(key, 4)
    shape = (N_NODE, node_tokens)
    drawn_slot = jnp.minimum(jax.random.randint(key_one, shape, 0, list_len), jax.random.randint(key_two, shape, 0, list_len))
    token_index = jnp.arange(node_tokens, dtype=jnp.int32)[None, :]
    drawn_slot = jnp.where(token_index < list_len, token_index % list_len, drawn_slot)
    slot_scores = jax.random.randint(key_three, (N_NODE, list_len), 0, 1 << 16) * list_len + jnp.arange(list_len, dtype=jnp.int32)[None, :]
    slot_order = lax.top_k(slot_scores, list_len)[1]
    mapped = jnp.take_along_axis(slot_order, drawn_slot, axis=1)
    token_scores = jax.random.randint(key_four, shape, 0, 1 << 16) * node_tokens + token_index
    token_order = lax.top_k(token_scores, node_tokens)[1]
    placed = jnp.take_along_axis(mapped, token_order, axis=1)
    return placed.reshape(-1).astype(jnp.int32)


def block_levels(stream_key, shape, pieces, least, top_value):
    gain = 1.0
    for dim, parts in pieces:
        draws = jax.random.uniform(jax.random.fold_in(jax.random.fold_in(stream_key, 6), dim), (parts,), jnp.float32, least / len(pieces), top_value / len(pieces))
        gain = gain * jnp.repeat(jnp.exp(draws), shape[dim] // parts).reshape((-1,) + (1,) * (len(shape) - 1 - dim))
    return gain


def centred(key, extent, deviation, most, pieces=(), kind=jnp.bfloat16):
    result = jax.random.normal(key, extent, jnp.float32) * deviation
    if len(pieces) > 0:
        result = block_levels(key, extent, pieces, -0.22, 0.18) * result
    return jnp.clip(result, min=-most, max=most).astype(kind)


def setup_inputs(seed: int = 0) -> dict:
    arg_keys = jax.random.split(jax.random.key(seed), 9)
    grads = centred(arg_keys[0], (TOKENS, D), 1.0, 6.0, ((0, 768),))
    token_slot = draw_token_slot(jax.random.fold_in(arg_keys[8], 71), 0)
    node_ids = draw_node_ids(jax.random.fold_in(arg_keys[8], 71), 0)
    touched_ids = draw_touched_ids(jax.random.fold_in(arg_keys[8], 71), 0)
    owner_map = draw_owner_map(jax.random.fold_in(arg_keys[8], 71), 0)
    moment = centred(arg_keys[5], (TOUCHED, D), 0.3, 4.0, ((0, 768),), jnp.float32)
    second = jnp.clip(jnp.exp(math.log(1.0) - 4.6051702 * jax.random.uniform(arg_keys[6], (TOUCHED, D), jnp.float32) ** block_levels(arg_keys[6], (TOUCHED, D), ((0, 768),), -0.2, 0.2)), 0.01, 1.0)
    master = centred(arg_keys[7], (TOUCHED, D), 0.02, 0.12, ((0, 768),), jnp.float32)
    return dict(grads=grads, token_slot=token_slot, node_ids=node_ids, touched_ids=touched_ids, owner_map=owner_map, moment=moment, second=second, master=master)


BETA_ONE = 0.9
BETA_TWO = 0.999
LEARN_RATE = 0.01
EPSILON = 1e-08

def adam_rows(gradient, moment, second, master, alive_rows):
    corr_one = 1.0 - BETA_ONE ** STEP
    corr_two = 1.0 - BETA_TWO ** STEP
    moment_new = BETA_ONE * moment + (1.0 - BETA_ONE) * gradient
    second_new = BETA_TWO * second + (1.0 - BETA_TWO) * gradient * gradient
    master_new = master - LEARN_RATE * (moment_new / corr_one) / (jnp.sqrt(second_new / corr_two) + EPSILON)
    kept = alive_rows[:, None]
    return (jnp.where(kept, moment_new, moment), jnp.where(kept, second_new, second), jnp.where(kept, master_new, master))

def reference(grads, token_slot, node_ids, touched_ids, owner_map, moment, second, master):
    list_len = N_LOCAL * SLOT_DEV
    grads_nodes = grads.reshape(N_NODE, N_LOCAL, TOK_DEV, D)
    slots_nodes = token_slot.reshape(N_NODE, N_LOCAL, TOK_DEV)

    def node_block(inputs):
        node_grads, node_slots = inputs

        def one_device(device_grads, device_slots):
            partial_sum = jax.ops.segment_sum(device_grads.astype(jnp.float32), device_slots, num_segments=list_len)
            return partial_sum.astype(jnp.bfloat16)
        partials = jax.vmap(one_device)(node_grads, node_slots)
        return lax.optimization_barrier(jnp.sum(partials.astype(jnp.float32), axis=0)).astype(jnp.bfloat16)
    node_sum = lax.map(node_block, (grads_nodes, slots_nodes))
    listed = node_ids.reshape(N_NODE, N_LOCAL, SLOT_DEV)
    owner_node = (listed // (VOCAB // N_NODE)).astype(jnp.int32)
    same_owner = owner_node[:, :, :, None] == owner_node[:, :, None, :]
    positions = jnp.arange(SLOT_DEV, dtype=jnp.int32)
    earlier = positions[None, :] < positions[:, None]
    rank_slot = lax.optimization_barrier(jnp.sum((same_owner & earlier[None, None]).astype(jnp.int32), axis=3))
    local_index = jnp.arange(N_LOCAL, dtype=jnp.int32)[None, :, None]
    node_index = jnp.arange(N_NODE, dtype=jnp.int32)[:, None, None]
    owner_device = owner_node * N_LOCAL + local_index
    touch_pos = owner_map[owner_device, node_index, rank_slot].astype(jnp.int32)
    target_row = (owner_device * TOUCH_CAP + touch_pos).reshape(-1).astype(jnp.int32)
    gradient = jax.ops.segment_sum(node_sum.reshape(-1, D).astype(jnp.float32), target_row, num_segments=N_NODE * N_LOCAL * TOUCH_CAP)
    moment_out, second_out, master_out = adam_rows(gradient, moment, second, master, touched_ids >= 0)
    fresh_rows = master_out.astype(jnp.bfloat16)
    slot_rows = fresh_rows[target_row]
    token_target = (jnp.arange(N_NODE, dtype=jnp.int32)[:, None] * list_len + slots_nodes.reshape(N_NODE, N_LOCAL * TOK_DEV)).reshape(-1).astype(jnp.int32)
    token_rows = slot_rows[token_target]
    return (token_rows, moment_out, second_out, master_out)
```

```python
import jax
import jax.numpy as jnp
from jax import lax
from jax.sharding import Mesh
from jax.sharding import PartitionSpec as P

VOCAB = 262144
STEP = 100


BETA_ONE = 0.9
BETA_TWO = 0.999
LEARN_RATE = 0.01
EPSILON = 1e-08

X_SIZE, Y_SIZE, Z_SIZE, CORES = 4, 8, 12, 2
FIRST_COLS = 2816

SWAP = [(0, 1), (1, 0)]


def adam_rows(gradient, moment, second, master, alive_rows):
    corr_one = 1.0 - BETA_ONE**STEP
    corr_two = 1.0 - BETA_TWO**STEP
    moment_new = BETA_ONE * moment + (1.0 - BETA_ONE) * gradient
    second_new = BETA_TWO * second + (1.0 - BETA_TWO) * gradient * gradient
    master_new = master - LEARN_RATE * (moment_new / corr_one) / (
        jnp.sqrt(second_new / corr_two) + EPSILON
    )
    kept = alive_rows[:, None]
    return (
        jnp.where(kept, moment_new, moment),
        jnp.where(kept, second_new, second),
        jnp.where(kept, master_new, master),
    )


def matches(rows, columns):
    return (rows[:, None] == columns[None, :]).astype(jnp.bfloat16)


def dot32(a, b):
    return jnp.dot(a, b, preferred_element_type=jnp.float32)


def on_device(grads, token_slot, node_ids, touched_ids, owner_map, moment, second, master):
    slot_dev = node_ids.shape[1]
    node_count = X_SIZE * Y_SIZE
    capacity = owner_map.shape[2]
    touch_cap = touched_ids.shape[0]
    core = lax.axis_index("c")
    place = lax.axis_index("z")

    other_slot = lax.ppermute(token_slot, "c", SWAP)

    def listed(z_of_row, core_index):
        k = lax.rem(lax.iota(jnp.int32, z_of_row.shape[0]), slot_dev)
        return (z_of_row * CORES + core_index) * slot_dev + k

    def partial_sum(rows, own, other):
        return (
            dot32(matches(rows, token_slot), own) + dot32(matches(rows, other_slot), other)
        ).astype(jnp.bfloat16)

    all_z = lax.div(lax.iota(jnp.int32, Z_SIZE * slot_dev), slot_dev)

    owner_node = node_ids[0] // (VOCAB // node_count)
    same_owner = owner_node[:, None] == owner_node[None, :]
    positions = lax.iota(jnp.int32, slot_dev)
    earlier = positions[None, :] < positions[:, None]
    rank_slot = jnp.sum((same_owner & earlier).astype(jnp.int32), axis=1)
    send_slot = owner_node * capacity + rank_slot
    route_map = matches(lax.iota(jnp.int32, node_count * capacity), send_slot)
    collect = matches(lax.iota(jnp.int32, touch_cap), owner_map.reshape(-1))

    def exchange(rows):
        width = rows.shape[1]
        return lax.all_to_all(
            rows.reshape(node_count, capacity, width),
            ("x", "y"),
            split_axis=0,
            concat_axis=0,
            tiled=True,
        ).reshape(node_count * capacity, width)

    def update(node_sum, columns):
        outgoing = dot32(route_map, node_sum).astype(jnp.bfloat16)
        gradient = dot32(collect, exchange(outgoing))
        states = adam_rows(
            gradient,
            moment[:, columns],
            second[:, columns],
            master[:, columns],
            touched_ids >= 0,
        )
        fresh_rows = states[2].astype(jnp.bfloat16)
        reply_rows = lax.dot_general(
            collect, fresh_rows, (((0,), (0,)), ((), ())), preferred_element_type=jnp.float32
        ).astype(jnp.bfloat16)
        returned = exchange(reply_rows)
        rows = lax.dot_general(
            route_map, returned, (((0,), (0,)), ((), ())), preferred_element_type=jnp.float32
        ).astype(jnp.bfloat16)
        return rows, states

    width = grads.shape[1]
    cols_a, cols_b = slice(0, FIRST_COLS), slice(FIRST_COLS, width)
    grads_a, grads_b = grads[:, cols_a], grads[:, cols_b]
    other_b = lax.ppermute(grads_b, "c", SWAP)
    other_a = lax.ppermute(grads_a, "c", SWAP)

    part_b = partial_sum(listed(all_z, core), grads_b, other_b)
    part_b, grads_a = lax.optimization_barrier((part_b, grads_a))
    sum_b = lax.psum_scatter(part_b, "z", scatter_dimension=0, tiled=True)

    part_a = partial_sum(listed(all_z, core), grads_a, other_a)
    blocks = lax.all_to_all(
        part_a.reshape(Z_SIZE, slot_dev, part_a.shape[1]),
        "z",
        split_axis=0,
        concat_axis=0,
        tiled=True,
    )
    sum_a = jnp.sum(blocks.astype(jnp.float32), axis=0).astype(jnp.bfloat16)

    rows_a, states_a = update(sum_a, cols_a)
    gathered_a = lax.all_gather(rows_a, ("z", "c"), axis=0, tiled=True)
    rows_b, states_b = update(sum_b, cols_b)
    own_b = lax.all_gather(rows_b, "z", axis=0, tiled=True)
    swapped_b = lax.ppermute(own_b, "c", SWAP)

    whole = lax.iota(jnp.int32, Z_SIZE * CORES * slot_dev)
    tokens_a = dot32(matches(token_slot, whole), gathered_a).astype(jnp.bfloat16)
    tokens_b = (
        dot32(matches(token_slot, listed(all_z, core)), own_b)
        + dot32(matches(token_slot, listed(all_z, 1 - core)), swapped_b)
    ).astype(jnp.bfloat16)
    moment_out, second_out, master_out = (
        jnp.concatenate([a, b], axis=1) for a, b in zip(states_a, states_b)
    )
    return (
        jnp.concatenate([tokens_a, tokens_b], axis=1),
        moment_out,
        second_out,
        master_out,
    )


def solution(mesh):
    axes = ("x", "y", "z", "c")
    fine = Mesh(mesh.devices.reshape(X_SIZE, Y_SIZE, Z_SIZE, CORES), axes)
    rows = P(axes, None)
    return jax.shard_map(
        on_device,
        mesh=fine,
        in_specs=(
            rows,
            P(axes),
            P(("x", "y"), ("z", "c")),
            P(axes),
            P(axes, None, None),
            rows,
            rows,
            rows,
        ),
        out_specs=(rows, rows, rows, rows),
        check_vma=False,
    )
```

```python
import jax
import jax.numpy as jnp
from jax import lax
from jax.sharding import Mesh
from jax.sharding import PartitionSpec as P

VOCAB = 262144
STEP = 100


BETA_ONE = 0.9
BETA_TWO = 0.999
LEARN_RATE = 0.01
EPSILON = 1e-08

X_SIZE, Y_SIZE, Z_SIZE, CORES = 4, 8, 12, 2
APART = 3
GROUP = Z_SIZE // APART
CHUNKS = 2

SWAP = [(0, 1), (1, 0)]


def shifted(steps):
    return [(i, (i + steps) % Z_SIZE) for i in range(Z_SIZE)]


def adam_rows(gradient, moment, second, master, alive_rows):
    corr_one = 1.0 - BETA_ONE**STEP
    corr_two = 1.0 - BETA_TWO**STEP
    moment_new = BETA_ONE * moment + (1.0 - BETA_ONE) * gradient
    second_new = BETA_TWO * second + (1.0 - BETA_TWO) * gradient * gradient
    master_new = master - LEARN_RATE * (moment_new / corr_one) / (
        jnp.sqrt(second_new / corr_two) + EPSILON
    )
    kept = alive_rows[:, None]
    return (
        jnp.where(kept, moment_new, moment),
        jnp.where(kept, second_new, second),
        jnp.where(kept, master_new, master),
    )


def matches(rows, columns):
    return (rows[:, None] == columns[None, :]).astype(jnp.bfloat16)


def dot32(a, b):
    return jnp.dot(a, b, preferred_element_type=jnp.float32)


def on_device(grads, token_slot, node_ids, touched_ids, owner_map, moment, second, master):
    slot_dev = node_ids.shape[1]
    node_count = X_SIZE * Y_SIZE
    capacity = owner_map.shape[2]
    touch_cap = touched_ids.shape[0]
    core = lax.axis_index("c")
    place = lax.axis_index("z")

    other_grads = lax.ppermute(grads, "c", SWAP)
    other_slot = lax.ppermute(token_slot, "c", SWAP)

    def rows_of(shift):
        row = lax.iota(jnp.int32, GROUP * slot_dev)
        z_of_row = lax.rem(place + (shift + Z_SIZE) + lax.div(row, slot_dev) * APART, Z_SIZE)
        return (z_of_row * CORES + core) * slot_dev + lax.rem(row, slot_dev)

    rows_here, rows_up, rows_down = rows_of(0), rows_of(1), rows_of(-1)

    def partial_sum(rows, columns):
        return (
            dot32(matches(rows, token_slot), grads[:, columns])
            + dot32(matches(rows, other_slot), other_grads[:, columns])
        ).astype(jnp.bfloat16)

    def node_sums(columns):
        from_down = lax.ppermute(partial_sum(rows_up, columns), "z", shifted(1))
        from_up = lax.ppermute(partial_sum(rows_down, columns), "z", shifted(-1))
        near = (
            partial_sum(rows_here, columns).astype(jnp.float32)
            + from_down.astype(jnp.float32)
            + from_up.astype(jnp.float32)
        ).astype(jnp.bfloat16)
        total = near[:slot_dev].astype(jnp.float32)
        for i in range(1, GROUP):
            block = near[i * slot_dev : (i + 1) * slot_dev]
            total = total + lax.ppermute(block, "z", shifted(i * APART)).astype(jnp.float32)
        return total.astype(jnp.bfloat16)

    owner_node = node_ids[0] // (VOCAB // node_count)
    same_owner = owner_node[:, None] == owner_node[None, :]
    positions = lax.iota(jnp.int32, slot_dev)
    earlier = positions[None, :] < positions[:, None]
    rank_slot = jnp.sum((same_owner & earlier).astype(jnp.int32), axis=1)
    position_map = owner_map.reshape(node_count, capacity)

    def send_places(kinds, kind):
        return (owner_node * kinds + kind) * capacity + rank_slot

    def touched_places(kinds, kind):
        unused = jnp.full_like(position_map, -1)
        return jnp.concatenate(
            [position_map if i == kind else unused for i in range(kinds)], axis=1
        ).reshape(-1)

    def exchange(rows):
        return lax.all_to_all(
            rows.reshape(node_count, -1, rows.shape[1]),
            ("x", "y"),
            split_axis=0,
            concat_axis=0,
            tiled=True,
        ).reshape(rows.shape)

    def to_owners(kinds, kind):
        places = lax.iota(jnp.int32, node_count * kinds * capacity)
        return matches(places, send_places(kinds, kind))

    def to_listers(kinds, kind):
        return matches(touched_places(kinds, kind), lax.iota(jnp.int32, touch_cap))

    def at_owner(received, kinds, kind):
        collect = matches(lax.iota(jnp.int32, touch_cap), touched_places(kinds, kind))
        return dot32(collect, received)

    def at_lister(received, kinds, kind):
        places = lax.iota(jnp.int32, node_count * kinds * capacity)
        return dot32(matches(send_places(kinds, kind), places), received).astype(jnp.bfloat16)

    def update(gradient, columns):
        states = adam_rows(
            gradient,
            moment[:, columns],
            second[:, columns],
            master[:, columns],
            touched_ids >= 0,
        )
        return states[2].astype(jnp.bfloat16), states

    listed = jnp.concatenate([rows_here, rows_down, rows_up])
    own_tokens = matches(token_slot, listed)
    other_tokens = matches(other_slot, listed)

    def token_parts(rows):
        here = jnp.concatenate(
            [rows] + [lax.ppermute(rows, "z", shifted(-i * APART)) for i in range(1, GROUP)]
        )
        from_down = lax.ppermute(here, "z", shifted(1))
        from_up = lax.ppermute(here, "z", shifted(-1))
        gathered = jnp.concatenate([here, from_down, from_up])
        theirs = dot32(other_tokens, gathered).astype(jnp.bfloat16)
        return dot32(own_tokens, gathered).astype(jnp.bfloat16) + lax.ppermute(theirs, "c", SWAP)

    step = grads.shape[1] // CHUNKS
    cols_a, cols_b = (slice(i * step, (i + 1) * step) for i in range(CHUNKS))

    sum_a = node_sums(cols_a)
    sum_b = node_sums(cols_b)
    received_a = exchange(dot32(to_owners(1, 0), sum_a).astype(jnp.bfloat16))
    fresh_a, states_a = update(at_owner(received_a, 1, 0), cols_a)
    received_both = exchange(
        (dot32(to_listers(2, 0), fresh_a) + dot32(to_owners(2, 1), sum_b)).astype(jnp.bfloat16)
    )
    tokens_a = token_parts(at_lister(received_both, 2, 0))
    fresh_b, states_b = update(at_owner(received_both, 2, 1), cols_b)
    received_b = exchange(dot32(to_listers(1, 0), fresh_b).astype(jnp.bfloat16))
    tokens_b = token_parts(at_lister(received_b, 1, 0))

    moment_out, second_out, master_out = (
        jnp.concatenate(parts, axis=1) for parts in zip(states_a, states_b)
    )
    return jnp.concatenate([tokens_a, tokens_b], axis=1), moment_out, second_out, master_out


def solution(mesh):
    axes = ("x", "y", "z", "c")
    fine = Mesh(mesh.devices.reshape(X_SIZE, Y_SIZE, Z_SIZE, CORES), axes)
    rows = P(axes, None)
    return jax.shard_map(
        on_device,
        mesh=fine,
        in_specs=(
            rows,
            P(axes),
            P(("x", "y"), ("z", "c")),
            P(axes),
            P(axes, None, None),
            rows,
            rows,
            rows,
        ),
        out_specs=(rows, rows, rows, rows),
        check_vma=False,
    )
```

```python
import jax
import jax.numpy as jnp
from jax import lax
from jax.experimental import pallas as pl
from jax.experimental.pallas import tpu as pltpu
from jax.sharding import Mesh
from jax.sharding import PartitionSpec as P

VOCAB = 262144
STEP = 100


BETA_ONE = 0.9
BETA_TWO = 0.999
LEARN_RATE = 0.01
EPSILON = 1e-08

X_SIZE, Y_SIZE, Z_SIZE, CORES = 4, 8, 12, 2
APART = 3
GROUP = Z_SIZE // APART
GROUPS = [[r + APART * k for k in range(GROUP)] for r in range(APART)]
BLOCK_COLS = 896

SWAP = [(0, 1), (1, 0)]


def shifted(steps):
    return [(i, (i + steps) % Z_SIZE) for i in range(Z_SIZE)]


def adam_rows(gradient, moment, second, master, alive_rows):
    corr_one = 1.0 - BETA_ONE**STEP
    corr_two = 1.0 - BETA_TWO**STEP
    moment_new = BETA_ONE * moment + (1.0 - BETA_ONE) * gradient
    second_new = BETA_TWO * second + (1.0 - BETA_TWO) * gradient * gradient
    master_new = master - LEARN_RATE * (moment_new / corr_one) / (
        jnp.sqrt(second_new / corr_two) + EPSILON
    )
    kept = alive_rows[:, None]
    return (
        jnp.where(kept, moment_new, moment),
        jnp.where(kept, second_new, second),
        jnp.where(kept, master_new, master),
    )


def matches(rows, columns):
    return (rows[:, None] == columns[None, :]).astype(jnp.bfloat16)


def dot32(a, b):
    return jnp.dot(a, b, preferred_element_type=jnp.float32)


def sum_kernel(rows_ref, own_slot_ref, other_slot_ref, own_ref, other_ref, *out_refs):
    rows = rows_ref[...]
    total = dot32((rows == own_slot_ref[...]).astype(jnp.bfloat16), own_ref[...])
    total += dot32((rows == other_slot_ref[...]).astype(jnp.bfloat16), other_ref[...])
    part = total.shape[0] // len(out_refs)
    for i, out_ref in enumerate(out_refs):
        out_ref[...] = total[i * part : (i + 1) * part].astype(out_ref.dtype)


def slot_sums(rows, own_slot, other_slot, own, other, parts):
    tokens, width = own.shape
    whole = lambda shape: pl.BlockSpec(shape, lambda i: (0, 0))
    columns = lambda height: pl.BlockSpec((height, BLOCK_COLS), lambda i: (0, i))
    part = rows.shape[0] // parts
    return pl.pallas_call(
        sum_kernel,
        grid=(width // BLOCK_COLS,),
        in_specs=[
            whole((rows.shape[0], 1)),
            whole((1, tokens)),
            whole((1, tokens)),
            columns(tokens),
            columns(tokens),
        ],
        out_specs=[columns(part)] * parts,
        out_shape=[jax.ShapeDtypeStruct((part, width), jnp.bfloat16)] * parts,
        cost_estimate=pl.CostEstimate(
            flops=4 * rows.shape[0] * tokens * width,
            bytes_accessed=2 * (2 * tokens + rows.shape[0]) * width,
            transcendentals=0,
        ),
        compiler_params=pltpu.CompilerParams(vmem_limit_bytes=16 * 2**20),
    )(rows[:, None], own_slot[None, :], other_slot[None, :], own, other)


def on_device(grads, token_slot, node_ids, touched_ids, owner_map, moment, second, master):
    slot_dev = node_ids.shape[1]
    width = grads.shape[1]
    node_count = X_SIZE * Y_SIZE
    capacity = owner_map.shape[2]
    touch_cap = touched_ids.shape[0]
    core = lax.axis_index("c")
    place = lax.axis_index("z")

    other_slot = lax.ppermute(token_slot, "c", SWAP)
    other_grads = lax.ppermute(grads, "c", SWAP)

    def rows_of(shift):
        row = lax.iota(jnp.int32, GROUP * slot_dev)
        z_of_row = lax.div(row, slot_dev) * APART + lax.rem(place + (shift + APART), APART)
        return (z_of_row * CORES + core) * slot_dev + lax.rem(row, slot_dev)

    listed = jnp.concatenate([rows_of(0), rows_of(-1), rows_of(1)])

    kept, for_down, for_up = slot_sums(listed, token_slot, other_slot, grads, other_grads, 3)
    from_down = lax.ppermute(for_up, "z", shifted(1))
    from_up = lax.ppermute(for_down, "z", shifted(-1))
    near = (
        kept.astype(jnp.float32) + from_down.astype(jnp.float32) + from_up.astype(jnp.float32)
    ).astype(jnp.bfloat16)
    blocks = lax.all_to_all(
        near.reshape(GROUP, slot_dev, width),
        "z",
        split_axis=0,
        concat_axis=0,
        tiled=True,
        axis_index_groups=GROUPS,
    )
    node_sum = jnp.sum(blocks.astype(jnp.float32), axis=0).astype(jnp.bfloat16)

    owner_node = node_ids[0] // (VOCAB // node_count)
    same_owner = owner_node[:, None] == owner_node[None, :]
    positions = lax.iota(jnp.int32, slot_dev)
    earlier = positions[None, :] < positions[:, None]
    rank_slot = jnp.sum((same_owner & earlier).astype(jnp.int32), axis=1)
    send_slot = owner_node * capacity + rank_slot
    send_places = lax.iota(jnp.int32, node_count * capacity)
    touched_places = lax.iota(jnp.int32, touch_cap)
    position_map = owner_map.reshape(-1)

    def exchange(rows):
        return lax.all_to_all(
            rows.astype(jnp.bfloat16).reshape(node_count, capacity, width),
            ("x", "y"),
            split_axis=0,
            concat_axis=0,
            tiled=True,
        ).reshape(node_count * capacity, width)

    incoming = exchange(dot32(matches(send_places, send_slot), node_sum))
    gradient = dot32(matches(touched_places, position_map), incoming)
    moment_out, second_out, master_out = adam_rows(
        gradient, moment, second, master, touched_ids >= 0
    )
    fresh_rows = master_out.astype(jnp.bfloat16)
    returned = exchange(dot32(matches(position_map, touched_places), fresh_rows))
    rows = dot32(matches(send_slot, send_places), returned).astype(jnp.bfloat16)

    here = lax.all_gather(rows, "z", axis=0, tiled=True, axis_index_groups=GROUPS)
    from_down = lax.ppermute(here, "z", shifted(1))
    from_up = lax.ppermute(here, "z", shifted(-1))
    gathered = jnp.concatenate([here, from_down, from_up])
    theirs = dot32(matches(other_slot, listed), gathered).astype(jnp.bfloat16)
    mine = dot32(matches(token_slot, listed), gathered).astype(jnp.bfloat16)
    token_rows = mine + lax.ppermute(theirs, "c", SWAP)
    return token_rows, moment_out, second_out, master_out


def solution(mesh):
    axes = ("x", "y", "z", "c")
    fine = Mesh(mesh.devices.reshape(X_SIZE, Y_SIZE, Z_SIZE, CORES), axes)
    rows = P(axes, None)
    return jax.shard_map(
        on_device,
        mesh=fine,
        in_specs=(
            rows,
            P(axes),
            P(("x", "y"), ("z", "c")),
            P(axes),
            P(axes, None, None),
            rows,
            rows,
            rows,
        ),
        out_specs=(rows, rows, rows, rows),
        check_vma=False,
    )
```

```python
import jax
import jax.numpy as jnp
from jax import lax
from jax.experimental import pallas as pl
from jax.experimental.pallas import tpu as pltpu
from jax.sharding import Mesh
from jax.sharding import PartitionSpec as P

VOCAB = 262144
STEP = 100


BETA_ONE = 0.9
BETA_TWO = 0.999
LEARN_RATE = 0.01
EPSILON = 1e-08

X_SIZE, Y_SIZE, Z_SIZE, CORES = 4, 8, 12, 2
APART = 3
GROUP = Z_SIZE // APART
GROUPS = [[r + APART * k for k in range(GROUP)] for r in range(APART)]
BLOCK_COLS = 896

SWAP = [(0, 1), (1, 0)]


def neighbour(steps):
    pairs = []
    for z in range(Z_SIZE):
        pairs.append((z * CORES, (z + steps) % Z_SIZE * CORES))
        pairs.append((z * CORES + 1, (z - steps) % Z_SIZE * CORES + 1))
    return pairs


def adam_rows(gradient, moment, second, master, alive_rows):
    corr_one = 1.0 - BETA_ONE**STEP
    corr_two = 1.0 - BETA_TWO**STEP
    moment_new = BETA_ONE * moment + (1.0 - BETA_ONE) * gradient
    second_new = BETA_TWO * second + (1.0 - BETA_TWO) * gradient * gradient
    master_new = master - LEARN_RATE * (moment_new / corr_one) / (
        jnp.sqrt(second_new / corr_two) + EPSILON
    )
    kept = alive_rows[:, None]
    return (
        jnp.where(kept, moment_new, moment),
        jnp.where(kept, second_new, second),
        jnp.where(kept, master_new, master),
    )


def matches(rows, columns):
    return (rows[:, None] == columns[None, :]).astype(jnp.bfloat16)


def dot32(a, b):
    return jnp.dot(a, b, preferred_element_type=jnp.float32)


def whole(shape):
    return pl.BlockSpec(shape, lambda i: (0, 0))


def columns(height):
    return pl.BlockSpec((height, BLOCK_COLS), lambda i: (0, i))


def own_kernel(rows_ref, slot_ref, tokens_ref, out_ref):
    chosen = (rows_ref[...] == slot_ref[...]).astype(jnp.bfloat16)
    out_ref[...] = dot32(chosen, tokens_ref[...])


def both_kernel(rows_ref, slot_ref, tokens_ref, own_ref, *out_refs):
    chosen = (rows_ref[...] == slot_ref[...]).astype(jnp.bfloat16)
    total = own_ref[...] + dot32(chosen, tokens_ref[...])
    part = total.shape[0] // len(out_refs)
    for i, out_ref in enumerate(out_refs):
        out_ref[...] = total[i * part : (i + 1) * part].astype(out_ref.dtype)


def slot_sums(rows, slots, tokens, own, parts):
    height, count, width = rows.shape[0], tokens.shape[0], tokens.shape[1]
    inputs = [rows[:, None], slots[None, :], tokens]
    in_specs = [whole((height, 1)), whole((1, count)), columns(count)]
    if own is None:
        kernel, out = own_kernel, [jax.ShapeDtypeStruct((height, width), jnp.float32)]
    else:
        kernel, out = both_kernel, [
            jax.ShapeDtypeStruct((height // parts, width), jnp.bfloat16) for _ in range(parts)
        ]
        inputs.append(own)
        in_specs.append(columns(height))
    results = pl.pallas_call(
        kernel,
        grid=(width // BLOCK_COLS,),
        in_specs=in_specs,
        out_specs=[columns(shape.shape[0]) for shape in out],
        out_shape=out,
        cost_estimate=pl.CostEstimate(
            flops=2 * height * count * width,
            bytes_accessed=(2 * count + 4 * height) * width,
            transcendentals=0,
        ),
        compiler_params=pltpu.CompilerParams(vmem_limit_bytes=16 * 2**20),
    )(*inputs)
    return results[0] if own is None else results


def on_device(grads, token_slot, node_ids, touched_ids, owner_map, moment, second, master):
    slot_dev = node_ids.shape[1]
    width = grads.shape[1]
    node_count = X_SIZE * Y_SIZE
    capacity = owner_map.shape[2]
    touch_cap = touched_ids.shape[0]
    core = lax.axis_index("c")
    place = lax.axis_index("z")

    other_grads = lax.ppermute(grads, "c", SWAP)
    other_slot = lax.ppermute(token_slot, "c", SWAP)

    def rows_of(shift):
        row = lax.iota(jnp.int32, GROUP * slot_dev)
        z_of_row = lax.div(row, slot_dev) * APART + lax.rem(place + (shift + APART), APART)
        return (z_of_row * CORES + core) * slot_dev + lax.rem(row, slot_dev)

    ahead = 1 - 2 * core
    listed = jnp.concatenate([rows_of(0), rows_of(ahead), rows_of(-ahead)])

    own_sums = slot_sums(listed, token_slot, grads, None, 1)
    kept, for_ahead, for_behind = slot_sums(listed, other_slot, other_grads, own_sums, 3)
    from_behind = lax.ppermute(for_ahead, ("z", "c"), neighbour(1))
    from_ahead = lax.ppermute(for_behind, ("z", "c"), neighbour(-1))
    near = (
        kept.astype(jnp.float32)
        + from_behind.astype(jnp.float32)
        + from_ahead.astype(jnp.float32)
    ).astype(jnp.bfloat16)
    blocks = lax.all_to_all(
        near.reshape(GROUP, slot_dev, width),
        "z",
        split_axis=0,
        concat_axis=0,
        tiled=True,
        axis_index_groups=GROUPS,
    )
    node_sum = jnp.sum(blocks.astype(jnp.float32), axis=0).astype(jnp.bfloat16)

    owner_node = node_ids[0] // (VOCAB // node_count)
    same_owner = owner_node[:, None] == owner_node[None, :]
    positions = lax.iota(jnp.int32, slot_dev)
    earlier = positions[None, :] < positions[:, None]
    rank_slot = jnp.sum((same_owner & earlier).astype(jnp.int32), axis=1)
    send_slot = owner_node * capacity + rank_slot
    send_places = lax.iota(jnp.int32, node_count * capacity)
    touched_places = lax.iota(jnp.int32, touch_cap)
    position_map = owner_map.reshape(-1)

    def exchange(rows):
        return lax.all_to_all(
            rows.astype(jnp.bfloat16).reshape(node_count, capacity, width),
            ("x", "y"),
            split_axis=0,
            concat_axis=0,
            tiled=True,
        ).reshape(node_count * capacity, width)

    incoming = exchange(dot32(matches(send_places, send_slot), node_sum))
    gradient = dot32(matches(touched_places, position_map), incoming)
    moment_out, second_out, master_out = adam_rows(
        gradient, moment, second, master, touched_ids >= 0
    )
    fresh_rows = master_out.astype(jnp.bfloat16)
    returned = exchange(dot32(matches(position_map, touched_places), fresh_rows))
    rows = dot32(matches(send_slot, send_places), returned).astype(jnp.bfloat16)

    here = lax.all_gather(rows, "z", axis=0, tiled=True, axis_index_groups=GROUPS)
    from_behind = lax.ppermute(here, ("z", "c"), neighbour(1))
    from_ahead = lax.ppermute(here, ("z", "c"), neighbour(-1))
    gathered = jnp.concatenate([here, from_ahead, from_behind])
    theirs = dot32(matches(other_slot, listed), gathered).astype(jnp.bfloat16)
    mine = dot32(matches(token_slot, listed), gathered).astype(jnp.bfloat16)
    token_rows = lax.optimization_barrier(mine) + lax.ppermute(theirs, "c", SWAP)
    return token_rows, moment_out, second_out, master_out


def solution(mesh):
    axes = ("x", "y", "z", "c")
    fine = Mesh(mesh.devices.reshape(X_SIZE, Y_SIZE, Z_SIZE, CORES), axes)
    rows = P(axes, None)
    return jax.shard_map(
        on_device,
        mesh=fine,
        in_specs=(
            rows,
            P(axes),
            P(("x", "y"), ("z", "c")),
            P(axes),
            P(axes, None, None),
            rows,
            rows,
            rows,
        ),
        out_specs=(rows, rows, rows, rows),
        check_vma=False,
    )
```

```python
import jax
import jax.numpy as jnp
from jax import lax
from jax.experimental import pallas as pl
from jax.experimental.pallas import tpu as pltpu
from jax.sharding import Mesh
from jax.sharding import PartitionSpec as P

VOCAB = 262144
STEP = 100


BETA_ONE = 0.9
BETA_TWO = 0.999
LEARN_RATE = 0.01
EPSILON = 1e-08

X_SIZE, Y_SIZE, Z_SIZE, CORES = 4, 8, 12, 2
APART = 3
GROUP = Z_SIZE // APART
GROUPS = [[r + APART * k for k in range(GROUP)] for r in range(APART)]
BLOCK_COLS = 896
KERNEL_VMEM = 56 * 2**20

SWAP = [(0, 1), (1, 0)]


def neighbour(steps):
    pairs = []
    for z in range(Z_SIZE):
        pairs.append((z * CORES, (z + steps) % Z_SIZE * CORES))
        pairs.append((z * CORES + 1, (z - steps) % Z_SIZE * CORES + 1))
    return pairs


def adam_rows(gradient, moment, second, master, alive_rows):
    corr_one = 1.0 - BETA_ONE**STEP
    corr_two = 1.0 - BETA_TWO**STEP
    moment_new = BETA_ONE * moment + (1.0 - BETA_ONE) * gradient
    second_new = BETA_TWO * second + (1.0 - BETA_TWO) * gradient * gradient
    master_new = master - LEARN_RATE * (moment_new / corr_one) / (
        jnp.sqrt(second_new / corr_two) + EPSILON
    )
    kept = alive_rows[:, None]
    return (
        jnp.where(kept, moment_new, moment),
        jnp.where(kept, second_new, second),
        jnp.where(kept, master_new, master),
    )


def matches(rows, columns):
    return (rows[:, None] == columns[None, :]).astype(jnp.bfloat16)


def dot32(a, b):
    return jnp.dot(a, b, preferred_element_type=jnp.float32)


def whole(shape):
    return pl.BlockSpec(shape, lambda i: (0, 0))


def columns(height):
    return pl.BlockSpec((height, BLOCK_COLS), lambda i: (0, i))


def sum_kernel(rows_ref, own_slot_ref, other_slot_ref, own_ref, other_ref, *out_refs):
    rows = rows_ref[...]
    total = dot32((rows == own_slot_ref[...]).astype(jnp.bfloat16), own_ref[...])
    total += dot32((rows == other_slot_ref[...]).astype(jnp.bfloat16), other_ref[...])
    part = total.shape[0] // len(out_refs)
    for i, out_ref in enumerate(out_refs):
        out_ref[...] = total[i * part : (i + 1) * part].astype(out_ref.dtype)


def slot_sums(rows, own_slot, other_slot, own, other, parts):
    height, count, width = rows.shape[0], own.shape[0], own.shape[1]
    part = height // parts
    return pl.pallas_call(
        sum_kernel,
        grid=(width // BLOCK_COLS,),
        in_specs=[
            whole((height, 1)),
            whole((1, count)),
            whole((1, count)),
            columns(count),
            columns(count),
        ],
        out_specs=[columns(part)] * parts,
        out_shape=[jax.ShapeDtypeStruct((part, width), jnp.bfloat16)] * parts,
        cost_estimate=pl.CostEstimate(
            flops=4 * height * count * width,
            bytes_accessed=2 * (2 * count + height) * width,
            transcendentals=0,
        ),
        compiler_params=pltpu.CompilerParams(vmem_limit_bytes=KERNEL_VMEM),
    )(rows[:, None], own_slot[None, :], other_slot[None, :], own, other)


def on_device(grads, token_slot, node_ids, touched_ids, owner_map, moment, second, master):
    slot_dev = node_ids.shape[1]
    width = grads.shape[1]
    node_count = X_SIZE * Y_SIZE
    capacity = owner_map.shape[2]
    touch_cap = touched_ids.shape[0]
    core = lax.axis_index("c")
    place = lax.axis_index("z")

    other_grads = lax.ppermute(grads, "c", SWAP)
    other_slot = lax.ppermute(token_slot, "c", SWAP)

    ahead = 1 - 2 * core

    def rows_of(shift, first_here):
        row = lax.iota(jnp.int32, GROUP * slot_dev)
        member = lax.div(row, slot_dev) * APART
        if first_here:
            z_of_row = lax.rem(place + shift + ahead * member + 2 * Z_SIZE, Z_SIZE)
        else:
            z_of_row = lax.rem(place + shift + APART, APART) + member
        return (z_of_row * CORES + core) * slot_dev + lax.rem(row, slot_dev)

    summed = jnp.concatenate([rows_of(shift, True) for shift in (0, ahead, -ahead)])
    kept, for_ahead, for_behind = slot_sums(
        summed, token_slot, other_slot, grads, other_grads, 3
    )
    from_behind = lax.ppermute(for_ahead, ("z", "c"), neighbour(1))
    from_ahead = lax.ppermute(for_behind, ("z", "c"), neighbour(-1))
    near = (
        kept.astype(jnp.float32)
        + from_behind.astype(jnp.float32)
        + from_ahead.astype(jnp.float32)
    ).astype(jnp.bfloat16)
    blocks = [near[i * slot_dev : (i + 1) * slot_dev] for i in range(GROUP)]
    total = blocks[0].astype(jnp.float32)
    for i in range(1, GROUP):
        total += lax.ppermute(blocks[i], ("z", "c"), neighbour(i * APART)).astype(jnp.float32)
    node_sum = total.astype(jnp.bfloat16)

    owner_node = node_ids[0] // (VOCAB // node_count)
    same_owner = owner_node[:, None] == owner_node[None, :]
    positions = lax.iota(jnp.int32, slot_dev)
    earlier = positions[None, :] < positions[:, None]
    rank_slot = jnp.sum((same_owner & earlier).astype(jnp.int32), axis=1)
    send_slot = owner_node * capacity + rank_slot
    send_places = lax.iota(jnp.int32, node_count * capacity)
    touched_places = lax.iota(jnp.int32, touch_cap)
    position_map = owner_map.reshape(-1)

    def exchange(rows):
        return lax.all_to_all(
            rows.astype(jnp.bfloat16).reshape(node_count, capacity, width),
            ("x", "y"),
            split_axis=0,
            concat_axis=0,
            tiled=True,
        ).reshape(node_count * capacity, width)

    incoming = exchange(dot32(matches(send_places, send_slot), node_sum))
    gradient = dot32(matches(touched_places, position_map), incoming)
    moment_out, second_out, master_out = adam_rows(
        gradient, moment, second, master, touched_ids >= 0
    )
    fresh_rows = master_out.astype(jnp.bfloat16)
    returned = exchange(dot32(matches(position_map, touched_places), fresh_rows))
    rows = dot32(matches(send_slot, send_places), returned).astype(jnp.bfloat16)

    listed = jnp.concatenate([rows_of(shift, False) for shift in (0, ahead, -ahead)])

    here = lax.all_gather(rows, "z", axis=0, tiled=True, axis_index_groups=GROUPS)
    from_behind = lax.ppermute(here, ("z", "c"), neighbour(1))
    from_ahead = lax.ppermute(here, ("z", "c"), neighbour(-1))
    gathered = jnp.concatenate([here, from_ahead, from_behind])
    theirs = dot32(matches(other_slot, listed), gathered).astype(jnp.bfloat16)
    mine = dot32(matches(token_slot, listed), gathered).astype(jnp.bfloat16)
    token_rows = lax.optimization_barrier(mine) + lax.ppermute(theirs, "c", SWAP)
    return token_rows, moment_out, second_out, master_out


def solution(mesh):
    axes = ("x", "y", "z", "c")
    fine = Mesh(mesh.devices.reshape(X_SIZE, Y_SIZE, Z_SIZE, CORES), axes)
    rows = P(axes, None)
    return jax.shard_map(
        on_device,
        mesh=fine,
        in_specs=(
            rows,
            P(axes),
            P(("x", "y"), ("z", "c")),
            P(axes),
            P(axes, None, None),
            rows,
            rows,
            rows,
        ),
        out_specs=(rows, rows, rows, rows),
        check_vma=False,
    )
```

```python
import jax
import jax.numpy as jnp
from jax import lax
from jax.experimental import pallas as pl
from jax.experimental.pallas import tpu as pltpu
from jax.sharding import Mesh
from jax.sharding import PartitionSpec as P

VOCAB = 262144
STEP = 100


BETA_ONE = 0.9
BETA_TWO = 0.999
LEARN_RATE = 0.01
EPSILON = 1e-08

X_SIZE, Y_SIZE, Z_SIZE, CORES = 4, 8, 12, 2
APART = 3
GROUP = Z_SIZE // APART
GROUPS = [[r + APART * k for k in range(GROUP)] for r in range(APART)]
BLOCK_COLS = 896
LAST_PARTS = 2

SWAP = [(0, 1), (1, 0)]


def neighbour(steps):
    pairs = []
    for z in range(Z_SIZE):
        pairs.append((z * CORES, (z + steps) % Z_SIZE * CORES))
        pairs.append((z * CORES + 1, (z - steps) % Z_SIZE * CORES + 1))
    return pairs


def adam_rows(gradient, moment, second, master, alive_rows):
    corr_one = 1.0 - BETA_ONE**STEP
    corr_two = 1.0 - BETA_TWO**STEP
    moment_new = BETA_ONE * moment + (1.0 - BETA_ONE) * gradient
    second_new = BETA_TWO * second + (1.0 - BETA_TWO) * gradient * gradient
    master_new = master - LEARN_RATE * (moment_new / corr_one) / (
        jnp.sqrt(second_new / corr_two) + EPSILON
    )
    kept = alive_rows[:, None]
    return (
        jnp.where(kept, moment_new, moment),
        jnp.where(kept, second_new, second),
        jnp.where(kept, master_new, master),
    )


def matches(rows, columns):
    return (rows[:, None] == columns[None, :]).astype(jnp.bfloat16)


def dot32(a, b):
    return jnp.dot(a, b, preferred_element_type=jnp.float32)


def sum_kernel(rows_ref, own_slot_ref, other_slot_ref, own_ref, other_ref, *out_refs):
    rows = rows_ref[...]
    own = (rows == own_slot_ref[...]).astype(jnp.bfloat16)
    other = (rows == other_slot_ref[...]).astype(jnp.bfloat16)
    part = rows.shape[0] // len(out_refs)
    for start in range(0, own_ref.shape[1], BLOCK_COLS):
        at = pl.ds(start, BLOCK_COLS)
        total = dot32(own, own_ref[:, at]) + dot32(other, other_ref[:, at])
        for i, out_ref in enumerate(out_refs):
            out_ref[:, at] = total[i * part : (i + 1) * part].astype(out_ref.dtype)


def slot_sums(rows, own_slot, other_slot, own, other, parts):
    height, count, width = rows.shape[0], own.shape[0], own.shape[1]
    in_vmem = pl.BlockSpec(memory_space=pltpu.VMEM)
    return pl.pallas_call(
        sum_kernel,
        in_specs=[in_vmem] * 5,
        out_specs=[in_vmem] * parts,
        out_shape=[jax.ShapeDtypeStruct((height // parts, width), jnp.bfloat16)] * parts,
        cost_estimate=pl.CostEstimate(
            flops=4 * height * count * width,
            bytes_accessed=2 * (2 * count + height) * width,
            transcendentals=0,
        ),
        compiler_params=pltpu.CompilerParams(vmem_limit_bytes=16 * 2**20),
    )(rows[:, None], own_slot[None, :], other_slot[None, :], own, other)


def on_device(grads, token_slot, node_ids, touched_ids, owner_map, moment, second, master):
    slot_dev = node_ids.shape[1]
    width = grads.shape[1]
    node_count = X_SIZE * Y_SIZE
    capacity = owner_map.shape[2]
    touch_cap = touched_ids.shape[0]
    core = lax.axis_index("c")
    place = lax.axis_index("z")

    other_grads = lax.ppermute(grads, "c", SWAP)
    other_slot = lax.ppermute(token_slot, "c", SWAP)

    ahead = 1 - 2 * core

    def rows_of(shift, first_here):
        row = lax.iota(jnp.int32, GROUP * slot_dev)
        member = lax.div(row, slot_dev) * APART
        if first_here:
            z_of_row = lax.rem(place + shift + ahead * member + 2 * Z_SIZE, Z_SIZE)
        else:
            z_of_row = lax.rem(place + shift + APART, APART) + member
        return (z_of_row * CORES + core) * slot_dev + lax.rem(row, slot_dev)

    summed = jnp.concatenate([rows_of(shift, True) for shift in (0, ahead, -ahead)])
    kept, for_ahead, for_behind = slot_sums(
        summed, token_slot, other_slot, grads, other_grads, 3
    )
    from_behind = lax.ppermute(for_ahead, ("z", "c"), neighbour(1))
    from_ahead = lax.ppermute(for_behind, ("z", "c"), neighbour(-1))
    near = (
        kept.astype(jnp.float32)
        + from_behind.astype(jnp.float32)
        + from_ahead.astype(jnp.float32)
    ).astype(jnp.bfloat16)
    blocks = [near[i * slot_dev : (i + 1) * slot_dev] for i in range(GROUP)]
    total = blocks[0].astype(jnp.float32)
    for i in range(1, GROUP):
        total += lax.ppermute(blocks[i], ("z", "c"), neighbour(i * APART)).astype(jnp.float32)
    node_sum = total.astype(jnp.bfloat16)

    owner_node = node_ids[0] // (VOCAB // node_count)
    same_owner = owner_node[:, None] == owner_node[None, :]
    positions = lax.iota(jnp.int32, slot_dev)
    earlier = positions[None, :] < positions[:, None]
    rank_slot = jnp.sum((same_owner & earlier).astype(jnp.int32), axis=1)
    send_slot = owner_node * capacity + rank_slot
    send_places = lax.iota(jnp.int32, node_count * capacity)
    touched_places = lax.iota(jnp.int32, touch_cap)
    position_map = owner_map.reshape(-1)

    def exchange(rows):
        return lax.all_to_all(
            rows.astype(jnp.bfloat16).reshape(node_count, capacity, width),
            ("x", "y"),
            split_axis=0,
            concat_axis=0,
            tiled=True,
        ).reshape(node_count * capacity, width)

    incoming = exchange(dot32(matches(send_places, send_slot), node_sum))
    gradient = dot32(matches(touched_places, position_map), incoming)
    moment_out, second_out, master_out = adam_rows(
        gradient, moment, second, master, touched_ids >= 0
    )
    fresh_rows = master_out.astype(jnp.bfloat16)
    returned = exchange(dot32(matches(position_map, touched_places), fresh_rows))
    rows = dot32(matches(send_slot, send_places), returned).astype(jnp.bfloat16)

    listed = jnp.concatenate([rows_of(shift, False) for shift in (0, ahead, -ahead)])

    here = lax.all_gather(rows, "z", axis=0, tiled=True, axis_index_groups=GROUPS)
    own_choice, other_choice = matches(token_slot, listed), matches(other_slot, listed)
    step = width // LAST_PARTS
    halves = [here[:, i * step : (i + 1) * step] for i in range(LAST_PARTS)]
    arrived = [
        (
            half,
            lax.ppermute(half, ("z", "c"), neighbour(-1)),
            lax.ppermute(half, ("z", "c"), neighbour(1)),
        )
        for half in halves
    ]
    tokens = []
    for gathered in map(jnp.concatenate, arrived):
        theirs = dot32(other_choice, gathered).astype(jnp.bfloat16)
        mine = dot32(own_choice, gathered).astype(jnp.bfloat16)
        tokens.append(lax.optimization_barrier(mine) + lax.ppermute(theirs, "c", SWAP))
    token_rows = jnp.concatenate(tokens, axis=1)
    return token_rows, moment_out, second_out, master_out


def solution(mesh):
    axes = ("x", "y", "z", "c")
    fine = Mesh(mesh.devices.reshape(X_SIZE, Y_SIZE, Z_SIZE, CORES), axes)
    rows = P(axes, None)
    return jax.shard_map(
        on_device,
        mesh=fine,
        in_specs=(
            rows,
            P(axes),
            P(("x", "y"), ("z", "c")),
            P(axes),
            P(axes, None, None),
            rows,
            rows,
            rows,
        ),
        out_specs=(rows, rows, rows, rows),
        check_vma=False,
    )
```

```python
import jax
import jax.numpy as jnp
from jax import lax
from jax.experimental import pallas as pl
from jax.experimental.pallas import tpu as pltpu
from jax.sharding import Mesh
from jax.sharding import PartitionSpec as P

VOCAB = 262144
STEP = 100


BETA_ONE = 0.9
BETA_TWO = 0.999
LEARN_RATE = 0.01
EPSILON = 1e-08

X_SIZE, Y_SIZE, Z_SIZE, CORES = 4, 8, 12, 2
SUM_APART = 4
APART = 3
GROUP = Z_SIZE // APART
GROUPS = [[r + APART * k for k in range(GROUP)] for r in range(APART)]
BLOCK_COLS = 896
LAST_PARTS = 2

SWAP = [(0, 1), (1, 0)]


def neighbour(steps):
    pairs = []
    for z in range(Z_SIZE):
        pairs.append((z * CORES, (z + steps) % Z_SIZE * CORES))
        pairs.append((z * CORES + 1, (z - steps) % Z_SIZE * CORES + 1))
    return pairs


def adam_rows(gradient, moment, second, master, alive_rows):
    corr_one = 1.0 - BETA_ONE**STEP
    corr_two = 1.0 - BETA_TWO**STEP
    moment_new = BETA_ONE * moment + (1.0 - BETA_ONE) * gradient
    second_new = BETA_TWO * second + (1.0 - BETA_TWO) * gradient * gradient
    master_new = master - LEARN_RATE * (moment_new / corr_one) / (
        jnp.sqrt(second_new / corr_two) + EPSILON
    )
    kept = alive_rows[:, None]
    return (
        jnp.where(kept, moment_new, moment),
        jnp.where(kept, second_new, second),
        jnp.where(kept, master_new, master),
    )


def matches(rows, columns):
    return (rows[:, None] == columns[None, :]).astype(jnp.bfloat16)


def dot32(a, b):
    return jnp.dot(a, b, preferred_element_type=jnp.float32)


def sum_kernel(rows_ref, own_slot_ref, other_slot_ref, own_ref, other_ref, *out_refs):
    rows = rows_ref[...]
    own = (rows == own_slot_ref[...]).astype(jnp.bfloat16)
    other = (rows == other_slot_ref[...]).astype(jnp.bfloat16)
    for start in range(0, own_ref.shape[1], BLOCK_COLS):
        at = pl.ds(start, BLOCK_COLS)
        total = dot32(own, own_ref[:, at]) + dot32(other, other_ref[:, at])
        first = 0
        for out_ref in out_refs:
            height = out_ref.shape[0]
            out_ref[:, at] = total[first : first + height].astype(out_ref.dtype)
            first += height


def slot_sums(rows, own_slot, other_slot, own, other, heights):
    count, width = own.shape
    in_vmem = pl.BlockSpec(memory_space=pltpu.VMEM)
    return pl.pallas_call(
        sum_kernel,
        in_specs=[in_vmem] * 5,
        out_specs=[in_vmem] * len(heights),
        out_shape=[jax.ShapeDtypeStruct((height, width), jnp.bfloat16) for height in heights],
        cost_estimate=pl.CostEstimate(
            flops=4 * rows.shape[0] * count * width,
            bytes_accessed=2 * (2 * count + rows.shape[0]) * width,
            transcendentals=0,
        ),
        compiler_params=pltpu.CompilerParams(vmem_limit_bytes=16 * 2**20),
    )(rows[:, None], own_slot[None, :], other_slot[None, :], own, other)


def on_device(grads, token_slot, node_ids, touched_ids, owner_map, moment, second, master):
    slot_dev = node_ids.shape[1]
    width = grads.shape[1]
    node_count = X_SIZE * Y_SIZE
    capacity = owner_map.shape[2]
    touch_cap = touched_ids.shape[0]
    core = lax.axis_index("c")
    place = lax.axis_index("z")

    other_grads = lax.ppermute(grads, "c", SWAP)
    other_slot = lax.ppermute(token_slot, "c", SWAP)

    ahead = 1 - 2 * core

    def rows_at(z_of_row):
        k = lax.rem(lax.iota(jnp.int32, z_of_row.shape[0]), slot_dev)
        return (z_of_row * CORES + core) * slot_dev + k

    def hub_rows(shift):
        block = lax.div(lax.iota(jnp.int32, Z_SIZE // SUM_APART * slot_dev), slot_dev)
        steps = shift + SUM_APART * block
        return rows_at(lax.rem(place + ahead * steps + 2 * Z_SIZE, Z_SIZE))

    def group_rows(shift):
        block = lax.div(lax.iota(jnp.int32, GROUP * slot_dev), slot_dev)
        return rows_at(lax.rem(place + ahead * shift + APART, APART) + APART * block)

    def send(rows, steps):
        return lax.ppermute(rows, ("z", "c"), neighbour(steps))

    def add(*terms):
        return sum(term.astype(jnp.float32) for term in terms)

    summed = jnp.concatenate([hub_rows(shift) for shift in (0, 1, -1, 2)])
    stay, move = slot_dev, (Z_SIZE // SUM_APART - 1) * slot_dev
    parts = slot_sums(summed, token_slot, other_slot, grads, other_grads, [stay, move] * 4)
    here, next_hub, last_hub, far_hub = zip(parts[::2], parts[1::2])

    def at_hub(part):
        relayed = send(far_hub[part], 1)
        from_ahead = send(last_hub[part], -1)
        from_behind = send(add(next_hub[part], relayed).astype(jnp.bfloat16), 1)
        return add(here[part], from_ahead, from_behind)

    moving = at_hub(1).astype(jnp.bfloat16)
    arrived = [
        send(moving[i * slot_dev : (i + 1) * slot_dev], (i + 1) * SUM_APART)
        for i in range(move // slot_dev)
    ]
    node_sum = add(at_hub(0), *arrived).astype(jnp.bfloat16)

    owner_node = node_ids[0] // (VOCAB // node_count)
    same_owner = owner_node[:, None] == owner_node[None, :]
    positions = lax.iota(jnp.int32, slot_dev)
    earlier = positions[None, :] < positions[:, None]
    rank_slot = jnp.sum((same_owner & earlier).astype(jnp.int32), axis=1)
    send_slot = owner_node * capacity + rank_slot
    send_places = lax.iota(jnp.int32, node_count * capacity)
    touched_places = lax.iota(jnp.int32, touch_cap)
    position_map = owner_map.reshape(-1)

    def exchange(rows):
        return lax.all_to_all(
            rows.astype(jnp.bfloat16).reshape(node_count, capacity, width),
            ("x", "y"),
            split_axis=0,
            concat_axis=0,
            tiled=True,
        ).reshape(node_count * capacity, width)

    incoming = exchange(dot32(matches(send_places, send_slot), node_sum))
    gradient = dot32(matches(touched_places, position_map), incoming)
    alive = touched_ids >= 0
    fresh_rows = adam_rows(gradient, moment, second, master, alive)[2].astype(jnp.bfloat16)
    states = adam_rows(lax.optimization_barrier(gradient), moment, second, master, alive)
    returned = exchange(dot32(matches(position_map, touched_places), fresh_rows))
    returned, moment_out, second_out, master_out = lax.optimization_barrier((returned, *states))
    rows = dot32(matches(send_slot, send_places), returned).astype(jnp.bfloat16)

    listed = jnp.concatenate([group_rows(shift) for shift in (0, 1, -1)])

    here = lax.all_gather(rows, "z", axis=0, tiled=True, axis_index_groups=GROUPS)
    own_choice, other_choice = matches(token_slot, listed), matches(other_slot, listed)
    step = width // LAST_PARTS
    halves = [here[:, i * step : (i + 1) * step] for i in range(LAST_PARTS)]
    arrived = [
        (
            half,
            send(half, -1),
            send(half, 1),
        )
        for half in halves
    ]
    tokens = []
    for gathered in map(jnp.concatenate, arrived):
        theirs = dot32(other_choice, gathered).astype(jnp.bfloat16)
        mine = dot32(own_choice, gathered).astype(jnp.bfloat16)
        tokens.append(lax.optimization_barrier(mine) + lax.ppermute(theirs, "c", SWAP))
    token_rows = jnp.concatenate(tokens, axis=1)
    return token_rows, moment_out, second_out, master_out


def solution(mesh):
    axes = ("x", "y", "z", "c")
    fine = Mesh(mesh.devices.reshape(X_SIZE, Y_SIZE, Z_SIZE, CORES), axes)
    rows = P(axes, None)
    return jax.shard_map(
        on_device,
        mesh=fine,
        in_specs=(
            rows,
            P(axes),
            P(("x", "y"), ("z", "c")),
            P(axes),
            P(axes, None, None),
            rows,
            rows,
            rows,
        ),
        out_specs=(rows, rows, rows, rows),
        check_vma=False,
    )
```

```python
import jax
import jax.numpy as jnp
from jax import lax
from jax.experimental import pallas as pl
from jax.experimental.pallas import tpu as pltpu
from jax.sharding import Mesh
from jax.sharding import PartitionSpec as P

VOCAB = 262144
STEP = 100


BETA_ONE = 0.9
BETA_TWO = 0.999
LEARN_RATE = 0.01
EPSILON = 1e-08

X_SIZE, Y_SIZE, Z_SIZE, CORES = 4, 8, 12, 2
SUM_APART = 4
APART = 3
GROUP = Z_SIZE // APART
GROUPS = [[r + APART * k for k in range(GROUP)] for r in range(APART)]
BLOCK_COLS = 896
LAST_PARTS = 2

SWAP = [(0, 1), (1, 0)]


def neighbour(steps):
    pairs = []
    for z in range(Z_SIZE):
        pairs.append((z * CORES, (z + steps) % Z_SIZE * CORES))
        pairs.append((z * CORES + 1, (z - steps) % Z_SIZE * CORES + 1))
    return pairs


def adam_rows(gradient, moment, second, master, alive_rows):
    corr_one = 1.0 - BETA_ONE**STEP
    corr_two = 1.0 - BETA_TWO**STEP
    moment_new = BETA_ONE * moment + (1.0 - BETA_ONE) * gradient
    second_new = BETA_TWO * second + (1.0 - BETA_TWO) * gradient * gradient
    master_new = master - LEARN_RATE * (moment_new / corr_one) / (
        jnp.sqrt(second_new / corr_two) + EPSILON
    )
    kept = alive_rows[:, None]
    return (
        jnp.where(kept, moment_new, moment),
        jnp.where(kept, second_new, second),
        jnp.where(kept, master_new, master),
    )


def matches(rows, columns):
    return (rows[:, None] == columns[None, :]).astype(jnp.bfloat16)


def dot32(a, b):
    return jnp.dot(a, b, preferred_element_type=jnp.float32)


def sum_kernel(rows_ref, own_slot_ref, other_slot_ref, own_ref, other_ref, *out_refs):
    rows = rows_ref[...]
    own = (rows == own_slot_ref[...]).astype(jnp.bfloat16)
    other = (rows == other_slot_ref[...]).astype(jnp.bfloat16)
    for start in range(0, own_ref.shape[1], BLOCK_COLS):
        at = pl.ds(start, BLOCK_COLS)
        total = dot32(own, own_ref[:, at]) + dot32(other, other_ref[:, at])
        first = 0
        for out_ref in out_refs:
            height = out_ref.shape[0]
            out_ref[:, at] = total[first : first + height].astype(out_ref.dtype)
            first += height


def slot_sums(rows, own_slot, other_slot, own, other, heights):
    count, width = own.shape
    in_vmem = pl.BlockSpec(memory_space=pltpu.VMEM)
    return pl.pallas_call(
        sum_kernel,
        in_specs=[in_vmem] * 5,
        out_specs=[in_vmem] * len(heights),
        out_shape=[jax.ShapeDtypeStruct((height, width), jnp.bfloat16) for height in heights],
        cost_estimate=pl.CostEstimate(
            flops=4 * rows.shape[0] * count * width,
            bytes_accessed=2 * (2 * count + rows.shape[0]) * width,
            transcendentals=0,
        ),
        compiler_params=pltpu.CompilerParams(vmem_limit_bytes=16 * 2**20),
    )(rows[:, None], own_slot[None, :], other_slot[None, :], own, other)


def on_device(grads, token_slot, node_ids, touched_ids, owner_map, moment, second, master):
    slot_dev = node_ids.shape[1]
    width = grads.shape[1]
    node_count = X_SIZE * Y_SIZE
    capacity = owner_map.shape[2]
    touch_cap = touched_ids.shape[0]
    core = lax.axis_index("c")
    place = lax.axis_index("z")

    other_grads = lax.ppermute(grads, "c", SWAP)
    other_slot = lax.ppermute(token_slot, "c", SWAP)

    ahead = 1 - 2 * core

    def rows_at(z_of_row):
        k = lax.rem(lax.iota(jnp.int32, z_of_row.shape[0]), slot_dev)
        return (z_of_row * CORES + core) * slot_dev + k

    def hub_rows(shift):
        block = lax.div(lax.iota(jnp.int32, Z_SIZE // SUM_APART * slot_dev), slot_dev)
        steps = shift + SUM_APART * block
        return rows_at(lax.rem(place + ahead * steps + 2 * Z_SIZE, Z_SIZE))

    def group_rows(shift):
        block = lax.div(lax.iota(jnp.int32, GROUP * slot_dev), slot_dev)
        return rows_at(lax.rem(place + ahead * shift + APART, APART) + APART * block)

    def send(rows, steps):
        return lax.ppermute(rows, ("z", "c"), neighbour(steps))

    def add(*terms):
        return sum(term.astype(jnp.float32) for term in terms)

    summed = jnp.concatenate([hub_rows(shift) for shift in (0, 1, -1, 2)])
    stay, move = slot_dev, (Z_SIZE // SUM_APART - 1) * slot_dev
    parts = slot_sums(summed, token_slot, other_slot, grads, other_grads, [stay, move] * 4)
    here, next_hub, last_hub, far_hub = zip(parts[::2], parts[1::2])

    relayed = send(far_hub[1], 1)
    from_ahead = send(last_hub[1], -1)
    relay_sum = add(next_hub[1], relayed).astype(jnp.bfloat16)
    relay_sum, held_back = lax.optimization_barrier((relay_sum, last_hub[0]))
    from_behind = send(relay_sum, 1)
    terms = []
    for i in range(move // slot_dev):
        at = slice(i * slot_dev, (i + 1) * slot_dev)
        block = add(here[1][at], from_ahead[at], from_behind[at]).astype(jnp.bfloat16)
        terms.append(send(block, (i + 1) * SUM_APART))
    terms += [here[0], send(held_back, -1)]
    terms.append(send(add(next_hub[0], send(far_hub[0], 1)).astype(jnp.bfloat16), 1))
    node_sum = add(*terms).astype(jnp.bfloat16)

    owner_node = node_ids[0] // (VOCAB // node_count)
    same_owner = owner_node[:, None] == owner_node[None, :]
    positions = lax.iota(jnp.int32, slot_dev)
    earlier = positions[None, :] < positions[:, None]
    rank_slot = jnp.sum((same_owner & earlier).astype(jnp.int32), axis=1)
    send_slot = owner_node * capacity + rank_slot
    send_places = lax.iota(jnp.int32, node_count * capacity)
    touched_places = lax.iota(jnp.int32, touch_cap)
    position_map = owner_map.reshape(-1)

    def exchange(rows):
        return lax.all_to_all(
            rows.astype(jnp.bfloat16).reshape(node_count, capacity, width),
            ("x", "y"),
            split_axis=0,
            concat_axis=0,
            tiled=True,
        ).reshape(node_count * capacity, width)

    incoming = exchange(dot32(matches(send_places, send_slot), node_sum))
    gradient = dot32(matches(touched_places, position_map), incoming)
    alive = touched_ids >= 0
    fresh_rows = adam_rows(gradient, moment, second, master, alive)[2].astype(jnp.bfloat16)
    states = adam_rows(lax.optimization_barrier(gradient), moment, second, master, alive)
    returned = exchange(dot32(matches(position_map, touched_places), fresh_rows))
    returned, moment_out, second_out, master_out = lax.optimization_barrier((returned, *states))
    rows = dot32(matches(send_slot, send_places), returned).astype(jnp.bfloat16)

    listed = jnp.concatenate([group_rows(shift) for shift in (0, 1, -1)])

    here = lax.all_gather(rows, "z", axis=0, tiled=True, axis_index_groups=GROUPS)
    own_choice, other_choice = matches(token_slot, listed), matches(other_slot, listed)
    step = width // LAST_PARTS
    halves = [here[:, i * step : (i + 1) * step] for i in range(LAST_PARTS)]
    arrived = [
        (
            half,
            send(half, -1),
            send(half, 1),
        )
        for half in halves
    ]
    tokens = []
    for gathered in map(jnp.concatenate, arrived):
        theirs = dot32(other_choice, gathered).astype(jnp.bfloat16)
        mine = dot32(own_choice, gathered).astype(jnp.bfloat16)
        tokens.append(lax.optimization_barrier(mine) + lax.ppermute(theirs, "c", SWAP))
    token_rows = jnp.concatenate(tokens, axis=1)
    return token_rows, moment_out, second_out, master_out


def solution(mesh):
    axes = ("x", "y", "z", "c")
    fine = Mesh(mesh.devices.reshape(X_SIZE, Y_SIZE, Z_SIZE, CORES), axes)
    rows = P(axes, None)
    return jax.shard_map(
        on_device,
        mesh=fine,
        in_specs=(
            rows,
            P(axes),
            P(("x", "y"), ("z", "c")),
            P(axes),
            P(axes, None, None),
            rows,
            rows,
            rows,
        ),
        out_specs=(rows, rows, rows, rows),
        check_vma=False,
    )
```

```python
import functools

import jax
import jax.numpy as jnp
from jax import lax
from jax.experimental import pallas as pl
from jax.experimental.pallas import tpu as pltpu
from jax.sharding import Mesh
from jax.sharding import PartitionSpec as P

VOCAB = 262144
STEP = 100


BETA_ONE = 0.9
BETA_TWO = 0.999
LEARN_RATE = 0.01
EPSILON = 1e-08

X_SIZE, Y_SIZE, Z_SIZE, CORES = 4, 8, 12, 2
SUM_APART = 4
APART = 3
GROUP = Z_SIZE // APART
GROUPS = [[r + APART * k for k in range(GROUP)] for r in range(APART)]
BLOCK_COLS = 896
LAST_PARTS = 2

SWAP = [(0, 1), (1, 0)]


def neighbour(steps):
    pairs = []
    for z in range(Z_SIZE):
        pairs.append((z * CORES, (z + steps) % Z_SIZE * CORES))
        pairs.append((z * CORES + 1, (z - steps) % Z_SIZE * CORES + 1))
    return pairs


def adam_rows(gradient, moment, second, master, alive_rows):
    corr_one = 1.0 - BETA_ONE**STEP
    corr_two = 1.0 - BETA_TWO**STEP
    moment_new = BETA_ONE * moment + (1.0 - BETA_ONE) * gradient
    second_new = BETA_TWO * second + (1.0 - BETA_TWO) * gradient * gradient
    master_new = master - LEARN_RATE * (moment_new / corr_one) / (
        jnp.sqrt(second_new / corr_two) + EPSILON
    )
    kept = alive_rows[:, None]
    return (
        jnp.where(kept, moment_new, moment),
        jnp.where(kept, second_new, second),
        jnp.where(kept, master_new, master),
    )


def matches(rows, columns):
    return (rows[:, None] == columns[None, :]).astype(jnp.bfloat16)


def dot32(a, b):
    return jnp.dot(a, b, preferred_element_type=jnp.float32)


def sum_kernel(count, has_base, rows_ref, *refs):
    pairs, refs = refs[: 2 * count], refs[2 * count :]
    base_ref, out_refs = (refs[0], refs[1:]) if has_base else (None, refs)
    rows = rows_ref[...]
    chosen = [(rows == slot_ref[...]).astype(jnp.bfloat16) for slot_ref in pairs[::2]]
    for start in range(0, pairs[1].shape[1], BLOCK_COLS):
        at = pl.ds(start, BLOCK_COLS)
        total = sum(dot32(a, ref[:, at]) for a, ref in zip(chosen, pairs[1::2]))
        if base_ref is not None:
            total += base_ref[:, at]
        first = 0
        for out_ref in out_refs:
            height = out_ref.shape[0]
            out_ref[:, at] = total[first : first + height].astype(out_ref.dtype)
            first += height


def slot_sums(rows, pairs, heights, base=None, out_dtype=jnp.bfloat16):
    count, width = pairs[0][1].shape
    operands = [rows[:, None]]
    for slots, tokens in pairs:
        operands += [slots[None, :], tokens]
    if base is not None:
        operands.append(base)
    in_vmem = pl.BlockSpec(memory_space=pltpu.VMEM)
    return pl.pallas_call(
        functools.partial(sum_kernel, len(pairs), base is not None),
        in_specs=[in_vmem] * len(operands),
        out_specs=[in_vmem] * len(heights),
        out_shape=[jax.ShapeDtypeStruct((height, width), out_dtype) for height in heights],
        cost_estimate=pl.CostEstimate(
            flops=2 * len(pairs) * rows.shape[0] * count * width,
            bytes_accessed=2 * (len(pairs) * count + rows.shape[0]) * width,
            transcendentals=0,
        ),
        compiler_params=pltpu.CompilerParams(vmem_limit_bytes=16 * 2**20),
    )(*operands)


def on_device(grads, token_slot, node_ids, touched_ids, owner_map, moment, second, master):
    slot_dev = node_ids.shape[1]
    width = grads.shape[1]
    node_count = X_SIZE * Y_SIZE
    capacity = owner_map.shape[2]
    touch_cap = touched_ids.shape[0]
    core = lax.axis_index("c")
    place = lax.axis_index("z")

    other_grads = lax.ppermute(grads, "c", SWAP)
    other_slot = lax.ppermute(token_slot, "c", SWAP)

    ahead = 1 - 2 * core

    def rows_at(z_of_row):
        k = lax.rem(lax.iota(jnp.int32, z_of_row.shape[0]), slot_dev)
        return (z_of_row * CORES + core) * slot_dev + k

    def hub_rows(shift):
        block = lax.div(lax.iota(jnp.int32, Z_SIZE // SUM_APART * slot_dev), slot_dev)
        steps = shift + SUM_APART * block
        return rows_at(lax.rem(place + ahead * steps + 2 * Z_SIZE, Z_SIZE))

    def group_rows(shift):
        block = lax.div(lax.iota(jnp.int32, GROUP * slot_dev), slot_dev)
        return rows_at(lax.rem(place + ahead * shift + APART, APART) + APART * block)

    def send(rows, steps):
        return lax.ppermute(rows, ("z", "c"), neighbour(steps))

    def add(*terms):
        return sum(term.astype(jnp.float32) for term in terms)

    stay, move = slot_dev, (Z_SIZE // SUM_APART - 1) * slot_dev
    here, next_hub, last_hub, far_hub = map(hub_rows, (0, 1, -1, 2))
    own, other = (token_slot, grads), (other_slot, other_grads)
    first = jnp.concatenate([far_hub[stay:], last_hub[stay:]])
    (own_first,) = slot_sums(first, [own], [2 * move], out_dtype=jnp.float32)
    far_move, last_move = slot_sums(first, [other], [move, move], own_first)
    later = jnp.concatenate([far_hub[:stay], last_hub[:stay], next_hub, here])
    far_move, last_move, later = lax.optimization_barrier((far_move, last_move, later))
    far_stay, last_stay, next_stay, next_move, here_stay, here_move = slot_sums(
        later, [own, other], [stay, stay, stay, move, stay, move]
    )

    relayed = send(far_move, 1)
    from_ahead = send(last_move, -1)
    relay_sum = add(next_move, relayed).astype(jnp.bfloat16)
    relay_sum, last_stay = lax.optimization_barrier((relay_sum, last_stay))
    from_behind = send(relay_sum, 1)
    terms = []
    for i in range(move // slot_dev):
        at = slice(i * slot_dev, (i + 1) * slot_dev)
        block = add(here_move[at], from_ahead[at], from_behind[at]).astype(jnp.bfloat16)
        terms.append(send(block, (i + 1) * SUM_APART))
    terms += [here_stay, send(last_stay, -1)]
    terms.append(send(add(next_stay, send(far_stay, 1)).astype(jnp.bfloat16), 1))
    node_sum = add(*terms).astype(jnp.bfloat16)

    owner_node = node_ids[0] // (VOCAB // node_count)
    same_owner = owner_node[:, None] == owner_node[None, :]
    positions = lax.iota(jnp.int32, slot_dev)
    earlier = positions[None, :] < positions[:, None]
    rank_slot = jnp.sum((same_owner & earlier).astype(jnp.int32), axis=1)
    send_slot = owner_node * capacity + rank_slot
    send_places = lax.iota(jnp.int32, node_count * capacity)
    touched_places = lax.iota(jnp.int32, touch_cap)
    position_map = owner_map.reshape(-1)

    def exchange(rows):
        return lax.all_to_all(
            rows.astype(jnp.bfloat16).reshape(node_count, capacity, width),
            ("x", "y"),
            split_axis=0,
            concat_axis=0,
            tiled=True,
        ).reshape(node_count * capacity, width)

    incoming = exchange(dot32(matches(send_places, send_slot), node_sum))
    gradient = dot32(matches(touched_places, position_map), incoming)
    alive = touched_ids >= 0
    fresh_rows = adam_rows(gradient, moment, second, master, alive)[2].astype(jnp.bfloat16)
    states = adam_rows(lax.optimization_barrier(gradient), moment, second, master, alive)
    returned = exchange(dot32(matches(position_map, touched_places), fresh_rows))
    returned, moment_out, second_out, master_out = lax.optimization_barrier((returned, *states))
    rows = dot32(matches(send_slot, send_places), returned).astype(jnp.bfloat16)

    listed = jnp.concatenate([group_rows(shift) for shift in (0, 1, -1)])

    here = lax.all_gather(rows, "z", axis=0, tiled=True, axis_index_groups=GROUPS)
    own_choice, other_choice = matches(token_slot, listed), matches(other_slot, listed)
    step = width // LAST_PARTS
    halves = [here[:, i * step : (i + 1) * step] for i in range(LAST_PARTS)]
    arrived = [
        (
            half,
            send(half, -1),
            send(half, 1),
        )
        for half in halves
    ]
    tokens = []
    for gathered in map(jnp.concatenate, arrived):
        theirs = dot32(other_choice, gathered).astype(jnp.bfloat16)
        mine = dot32(own_choice, gathered).astype(jnp.bfloat16)
        tokens.append(lax.optimization_barrier(mine) + lax.ppermute(theirs, "c", SWAP))
    token_rows = jnp.concatenate(tokens, axis=1)
    return token_rows, moment_out, second_out, master_out


def solution(mesh):
    axes = ("x", "y", "z", "c")
    fine = Mesh(mesh.devices.reshape(X_SIZE, Y_SIZE, Z_SIZE, CORES), axes)
    rows = P(axes, None)
    return jax.shard_map(
        on_device,
        mesh=fine,
        in_specs=(
            rows,
            P(axes),
            P(("x", "y"), ("z", "c")),
            P(axes),
            P(axes, None, None),
            rows,
            rows,
            rows,
        ),
        out_specs=(rows, rows, rows, rows),
        check_vma=False,
    )
```

```python
import functools

import jax
import jax.numpy as jnp
from jax import lax
from jax.experimental import pallas as pl
from jax.experimental.pallas import tpu as pltpu
from jax.sharding import Mesh
from jax.sharding import PartitionSpec as P

VOCAB = 262144
STEP = 100


BETA_ONE = 0.9
BETA_TWO = 0.999
LEARN_RATE = 0.01
EPSILON = 1e-08

X_SIZE, Y_SIZE, Z_SIZE, CORES = 4, 8, 12, 2
SUM_APART = 4
APART = 3
GROUP = Z_SIZE // APART
GROUPS = [[r + APART * k for k in range(GROUP)] for r in range(APART)]
BLOCK_COLS = 896
LAST_PARTS = 2

SWAP = [(0, 1), (1, 0)]


def neighbour(steps):
    pairs = []
    for z in range(Z_SIZE):
        pairs.append((z * CORES, (z + steps) % Z_SIZE * CORES))
        pairs.append((z * CORES + 1, (z - steps) % Z_SIZE * CORES + 1))
    return pairs


def adam_rows(gradient, moment, second, master, alive_rows):
    corr_one = 1.0 - BETA_ONE**STEP
    corr_two = 1.0 - BETA_TWO**STEP
    moment_new = BETA_ONE * moment + (1.0 - BETA_ONE) * gradient
    second_new = BETA_TWO * second + (1.0 - BETA_TWO) * gradient * gradient
    master_new = master - LEARN_RATE * (moment_new / corr_one) / (
        jnp.sqrt(second_new / corr_two) + EPSILON
    )
    kept = alive_rows[:, None]
    return (
        jnp.where(kept, moment_new, moment),
        jnp.where(kept, second_new, second),
        jnp.where(kept, master_new, master),
    )


def matches(rows, columns):
    return (rows[:, None] == columns[None, :]).astype(jnp.bfloat16)


def dot32(a, b):
    return jnp.dot(a, b, preferred_element_type=jnp.float32)


def sum_kernel(rows_ref, own_slot_ref, other_slot_ref, own_ref, other_ref, *out_refs):
    rows = rows_ref[...]
    own = (rows == own_slot_ref[...]).astype(jnp.bfloat16)
    other = (rows == other_slot_ref[...]).astype(jnp.bfloat16)
    for start in range(0, own_ref.shape[1], BLOCK_COLS):
        at = pl.ds(start, BLOCK_COLS)
        total = dot32(own, own_ref[:, at]) + dot32(other, other_ref[:, at])
        first = 0
        for out_ref in out_refs:
            height = out_ref.shape[0]
            out_ref[:, at] = total[first : first + height].astype(out_ref.dtype)
            first += height


def slot_sums(rows, own_slot, other_slot, own, other, heights):
    count, width = own.shape
    in_vmem = pl.BlockSpec(memory_space=pltpu.VMEM)
    return pl.pallas_call(
        sum_kernel,
        in_specs=[in_vmem] * 5,
        out_specs=[in_vmem] * len(heights),
        out_shape=[jax.ShapeDtypeStruct((height, width), jnp.bfloat16) for height in heights],
        cost_estimate=pl.CostEstimate(
            flops=4 * rows.shape[0] * count * width,
            bytes_accessed=2 * (2 * count + rows.shape[0]) * width,
            transcendentals=0,
        ),
        compiler_params=pltpu.CompilerParams(vmem_limit_bytes=16 * 2**20),
    )(rows[:, None], own_slot[None, :], other_slot[None, :], own, other)


def place_kernel(start, mine_ref, theirs_ref, *refs):
    whole_ref, held, done = refs[-3:]
    held[...] = mine_ref[...] + theirs_ref[...]
    at = pl.ds(start, held.shape[1])
    copy = pltpu.make_async_copy(held, whole_ref.at[:, at], done)
    copy.start()
    copy.wait()


def place_sum(mine, theirs, start, width, whole=None):
    in_vmem, in_hbm = pl.BlockSpec(memory_space=pltpu.VMEM), pl.BlockSpec(memory_space=pltpu.HBM)
    operands = [mine, theirs] + ([] if whole is None else [whole])
    return pl.pallas_call(
        functools.partial(place_kernel, start),
        in_specs=[in_vmem, in_vmem] + [in_hbm] * (len(operands) - 2),
        out_specs=in_hbm,
        out_shape=jax.ShapeDtypeStruct((mine.shape[0], width), mine.dtype),
        scratch_shapes=[pltpu.VMEM(mine.shape, mine.dtype), pltpu.SemaphoreType.DMA],
        input_output_aliases={} if whole is None else {2: 0},
        cost_estimate=pl.CostEstimate(
            flops=mine.size, bytes_accessed=6 * mine.size, transcendentals=0
        ),
        compiler_params=pltpu.CompilerParams(vmem_limit_bytes=16 * 2**20),
    )(*operands)


def on_device(grads, token_slot, node_ids, touched_ids, owner_map, moment, second, master):
    slot_dev = node_ids.shape[1]
    width = grads.shape[1]
    node_count = X_SIZE * Y_SIZE
    capacity = owner_map.shape[2]
    touch_cap = touched_ids.shape[0]
    core = lax.axis_index("c")
    place = lax.axis_index("z")

    other_grads = lax.ppermute(grads, "c", SWAP)
    other_slot = lax.ppermute(token_slot, "c", SWAP)

    ahead = 1 - 2 * core

    def rows_at(z_of_row):
        k = lax.rem(lax.iota(jnp.int32, z_of_row.shape[0]), slot_dev)
        return (z_of_row * CORES + core) * slot_dev + k

    def hub_rows(shift):
        block = lax.div(lax.iota(jnp.int32, Z_SIZE // SUM_APART * slot_dev), slot_dev)
        steps = shift + SUM_APART * block
        return rows_at(lax.rem(place + ahead * steps + 2 * Z_SIZE, Z_SIZE))

    def group_rows(shift):
        block = lax.div(lax.iota(jnp.int32, GROUP * slot_dev), slot_dev)
        return rows_at(lax.rem(place + ahead * shift + APART, APART) + APART * block)

    def send(rows, steps):
        return lax.ppermute(rows, ("z", "c"), neighbour(steps))

    def add(*terms):
        return sum(term.astype(jnp.float32) for term in terms)

    summed = jnp.concatenate([hub_rows(shift) for shift in (0, 1, -1, 2)])
    stay, move = slot_dev, (Z_SIZE // SUM_APART - 1) * slot_dev
    parts = slot_sums(summed, token_slot, other_slot, grads, other_grads, [stay, move] * 4)
    here, next_hub, last_hub, far_hub = zip(parts[::2], parts[1::2])

    relayed = send(far_hub[1], 1)
    from_ahead = send(last_hub[1], -1)
    relay_sum = add(next_hub[1], relayed).astype(jnp.bfloat16)
    relay_sum, held_back = lax.optimization_barrier((relay_sum, last_hub[0]))
    from_behind = send(relay_sum, 1)
    terms = []
    for i in range(move // slot_dev):
        at = slice(i * slot_dev, (i + 1) * slot_dev)
        block = add(here[1][at], from_ahead[at], from_behind[at]).astype(jnp.bfloat16)
        terms.append(send(block, (i + 1) * SUM_APART))
    terms += [here[0], send(held_back, -1)]
    terms.append(send(add(next_hub[0], send(far_hub[0], 1)).astype(jnp.bfloat16), 1))
    node_sum = add(*terms).astype(jnp.bfloat16)

    owner_node = node_ids[0] // (VOCAB // node_count)
    same_owner = owner_node[:, None] == owner_node[None, :]
    positions = lax.iota(jnp.int32, slot_dev)
    earlier = positions[None, :] < positions[:, None]
    rank_slot = jnp.sum((same_owner & earlier).astype(jnp.int32), axis=1)
    send_slot = owner_node * capacity + rank_slot
    send_places = lax.iota(jnp.int32, node_count * capacity)
    touched_places = lax.iota(jnp.int32, touch_cap)
    position_map = owner_map.reshape(-1)

    def exchange(rows):
        return lax.all_to_all(
            rows.astype(jnp.bfloat16).reshape(node_count, capacity, width),
            ("x", "y"),
            split_axis=0,
            concat_axis=0,
            tiled=True,
        ).reshape(node_count * capacity, width)

    incoming = exchange(dot32(matches(send_places, send_slot), node_sum))
    gradient = dot32(matches(touched_places, position_map), incoming)
    alive = touched_ids >= 0
    fresh_rows = adam_rows(gradient, moment, second, master, alive)[2].astype(jnp.bfloat16)
    states = adam_rows(lax.optimization_barrier(gradient), moment, second, master, alive)
    returned = exchange(dot32(matches(position_map, touched_places), fresh_rows))
    returned, moment_out, second_out, master_out = lax.optimization_barrier((returned, *states))
    rows = dot32(matches(send_slot, send_places), returned).astype(jnp.bfloat16)

    listed = jnp.concatenate([group_rows(shift) for shift in (0, 1, -1)])

    here = lax.all_gather(rows, "z", axis=0, tiled=True, axis_index_groups=GROUPS)
    own_choice, other_choice = matches(token_slot, listed), matches(other_slot, listed)
    step = width // LAST_PARTS
    halves = [here[:, i * step : (i + 1) * step] for i in range(LAST_PARTS)]
    arrived = [
        (
            half,
            send(half, -1),
            send(half, 1),
        )
        for half in halves
    ]
    token_rows = None
    for i, gathered in enumerate(map(jnp.concatenate, arrived)):
        theirs = dot32(other_choice, gathered).astype(jnp.bfloat16)
        mine = dot32(own_choice, gathered).astype(jnp.bfloat16)
        theirs = lax.ppermute(theirs, "c", SWAP)
        token_rows = place_sum(mine, theirs, i * step, width, token_rows)
    return token_rows, moment_out, second_out, master_out


def solution(mesh):
    axes = ("x", "y", "z", "c")
    fine = Mesh(mesh.devices.reshape(X_SIZE, Y_SIZE, Z_SIZE, CORES), axes)
    rows = P(axes, None)
    return jax.shard_map(
        on_device,
        mesh=fine,
        in_specs=(
            rows,
            P(axes),
            P(("x", "y"), ("z", "c")),
            P(axes),
            P(axes, None, None),
            rows,
            rows,
            rows,
        ),
        out_specs=(rows, rows, rows, rows),
        check_vma=False,
    )
```

```python
import functools

import jax
import jax.numpy as jnp
from jax import lax
from jax.experimental import pallas as pl
from jax.experimental.pallas import tpu as pltpu
from jax.sharding import Mesh
from jax.sharding import PartitionSpec as P

VOCAB = 262144
STEP = 100


BETA_ONE = 0.9
BETA_TWO = 0.999
LEARN_RATE = 0.01
EPSILON = 1e-08

X_SIZE, Y_SIZE, Z_SIZE, CORES = 4, 8, 12, 2
SUM_APART = 4
APART = 3
GROUP = Z_SIZE // APART
GROUPS = [[r + APART * k for k in range(GROUP)] for r in range(APART)]
BLOCK_COLS = 896
LAST_CUTS = (0, 3584, 5376)

SWAP = [(0, 1), (1, 0)]


def neighbour(steps):
    pairs = []
    for z in range(Z_SIZE):
        pairs.append((z * CORES, (z + steps) % Z_SIZE * CORES))
        pairs.append((z * CORES + 1, (z - steps) % Z_SIZE * CORES + 1))
    return pairs


def adam_rows(gradient, moment, second, master, alive_rows):
    corr_one = 1.0 - BETA_ONE**STEP
    corr_two = 1.0 - BETA_TWO**STEP
    moment_new = BETA_ONE * moment + (1.0 - BETA_ONE) * gradient
    second_new = BETA_TWO * second + (1.0 - BETA_TWO) * gradient * gradient
    master_new = master - LEARN_RATE * (moment_new / corr_one) / (
        jnp.sqrt(second_new / corr_two) + EPSILON
    )
    kept = alive_rows[:, None]
    return (
        jnp.where(kept, moment_new, moment),
        jnp.where(kept, second_new, second),
        jnp.where(kept, master_new, master),
    )


def matches(rows, columns):
    return (rows[:, None] == columns[None, :]).astype(jnp.bfloat16)


def dot32(a, b):
    return jnp.dot(a, b, preferred_element_type=jnp.float32)


def sum_kernel(rows_ref, own_slot_ref, other_slot_ref, own_ref, other_ref, *out_refs):
    rows = rows_ref[...]
    own = (rows == own_slot_ref[...]).astype(jnp.bfloat16)
    other = (rows == other_slot_ref[...]).astype(jnp.bfloat16)
    for start in range(0, own_ref.shape[1], BLOCK_COLS):
        at = pl.ds(start, BLOCK_COLS)
        total = dot32(own, own_ref[:, at]) + dot32(other, other_ref[:, at])
        first = 0
        for out_ref in out_refs:
            height = out_ref.shape[0]
            out_ref[:, at] = total[first : first + height].astype(out_ref.dtype)
            first += height


def slot_sums(rows, own_slot, other_slot, own, other, heights):
    count, width = own.shape
    in_vmem = pl.BlockSpec(memory_space=pltpu.VMEM)
    return pl.pallas_call(
        sum_kernel,
        in_specs=[in_vmem] * 5,
        out_specs=[in_vmem] * len(heights),
        out_shape=[jax.ShapeDtypeStruct((height, width), jnp.bfloat16) for height in heights],
        cost_estimate=pl.CostEstimate(
            flops=4 * rows.shape[0] * count * width,
            bytes_accessed=2 * (2 * count + rows.shape[0]) * width,
            transcendentals=0,
        ),
        compiler_params=pltpu.CompilerParams(vmem_limit_bytes=16 * 2**20),
    )(rows[:, None], own_slot[None, :], other_slot[None, :], own, other)


def place_kernel(start, mine_ref, theirs_ref, *refs):
    whole_ref, held, done = refs[-3:]
    held[...] = mine_ref[...] + theirs_ref[...]
    at = pl.ds(start, held.shape[1])
    copy = pltpu.make_async_copy(held, whole_ref.at[:, at], done)
    copy.start()
    copy.wait()


def place_sum(mine, theirs, start, width, whole=None):
    in_vmem, in_hbm = pl.BlockSpec(memory_space=pltpu.VMEM), pl.BlockSpec(memory_space=pltpu.HBM)
    operands = [mine, theirs] + ([] if whole is None else [whole])
    return pl.pallas_call(
        functools.partial(place_kernel, start),
        in_specs=[in_vmem, in_vmem] + [in_hbm] * (len(operands) - 2),
        out_specs=in_hbm,
        out_shape=jax.ShapeDtypeStruct((mine.shape[0], width), mine.dtype),
        scratch_shapes=[pltpu.VMEM(mine.shape, mine.dtype), pltpu.SemaphoreType.DMA],
        input_output_aliases={} if whole is None else {2: 0},
        cost_estimate=pl.CostEstimate(
            flops=mine.size, bytes_accessed=6 * mine.size, transcendentals=0
        ),
        compiler_params=pltpu.CompilerParams(vmem_limit_bytes=16 * 2**20),
    )(*operands)


def on_device(grads, token_slot, node_ids, touched_ids, owner_map, moment, second, master):
    slot_dev = node_ids.shape[1]
    width = grads.shape[1]
    node_count = X_SIZE * Y_SIZE
    capacity = owner_map.shape[2]
    touch_cap = touched_ids.shape[0]
    core = lax.axis_index("c")
    place = lax.axis_index("z")

    other_grads = lax.ppermute(grads, "c", SWAP)
    other_slot = lax.ppermute(token_slot, "c", SWAP)

    ahead = 1 - 2 * core

    def rows_at(z_of_row):
        k = lax.rem(lax.iota(jnp.int32, z_of_row.shape[0]), slot_dev)
        return (z_of_row * CORES + core) * slot_dev + k

    def hub_rows(shift):
        block = lax.div(lax.iota(jnp.int32, Z_SIZE // SUM_APART * slot_dev), slot_dev)
        steps = shift + SUM_APART * block
        return rows_at(lax.rem(place + ahead * steps + 2 * Z_SIZE, Z_SIZE))

    def group_rows(shift):
        block = lax.div(lax.iota(jnp.int32, GROUP * slot_dev), slot_dev)
        return rows_at(lax.rem(place + ahead * shift + APART, APART) + APART * block)

    def send(rows, steps):
        return lax.ppermute(rows, ("z", "c"), neighbour(steps))

    def add(*terms):
        return sum(term.astype(jnp.float32) for term in terms)

    summed = jnp.concatenate([hub_rows(shift) for shift in (0, 1, -1, 2)])
    stay, move = slot_dev, (Z_SIZE // SUM_APART - 1) * slot_dev
    parts = slot_sums(summed, token_slot, other_slot, grads, other_grads, [stay, move] * 4)
    here, next_hub, last_hub, far_hub = zip(parts[::2], parts[1::2])

    relayed = send(far_hub[1], 1)
    from_ahead = send(last_hub[1], -1)
    relay_sum = add(next_hub[1], relayed).astype(jnp.bfloat16)
    relay_sum, held_back = lax.optimization_barrier((relay_sum, last_hub[0]))
    from_behind = send(relay_sum, 1)
    terms = []
    for i in range(move // slot_dev):
        at = slice(i * slot_dev, (i + 1) * slot_dev)
        block = add(here[1][at], from_ahead[at], from_behind[at]).astype(jnp.bfloat16)
        terms.append(send(block, (i + 1) * SUM_APART))
    terms += [here[0], send(held_back, -1)]
    terms.append(send(add(next_hub[0], send(far_hub[0], 1)).astype(jnp.bfloat16), 1))
    node_sum = add(*terms).astype(jnp.bfloat16)

    owner_node = node_ids[0] // (VOCAB // node_count)
    same_owner = owner_node[:, None] == owner_node[None, :]
    positions = lax.iota(jnp.int32, slot_dev)
    earlier = positions[None, :] < positions[:, None]
    rank_slot = jnp.sum((same_owner & earlier).astype(jnp.int32), axis=1)
    send_slot = owner_node * capacity + rank_slot
    send_places = lax.iota(jnp.int32, node_count * capacity)
    touched_places = lax.iota(jnp.int32, touch_cap)
    position_map = owner_map.reshape(-1)

    def exchange(rows):
        return lax.all_to_all(
            rows.astype(jnp.bfloat16).reshape(node_count, capacity, width),
            ("x", "y"),
            split_axis=0,
            concat_axis=0,
            tiled=True,
        ).reshape(node_count * capacity, width)

    incoming = exchange(dot32(matches(send_places, send_slot), node_sum))
    gradient = dot32(matches(touched_places, position_map), incoming)
    alive = touched_ids >= 0
    fresh_rows = adam_rows(gradient, moment, second, master, alive)[2].astype(jnp.bfloat16)
    states = adam_rows(lax.optimization_barrier(gradient), moment, second, master, alive)
    returned = exchange(dot32(matches(position_map, touched_places), fresh_rows))
    returned, moment_out, second_out, master_out = lax.optimization_barrier((returned, *states))
    rows = dot32(matches(send_slot, send_places), returned).astype(jnp.bfloat16)

    listed = jnp.concatenate([group_rows(shift) for shift in (0, 1, -1)])

    here = lax.all_gather(rows, "z", axis=0, tiled=True, axis_index_groups=GROUPS)
    own_choice, other_choice = matches(token_slot, listed), matches(other_slot, listed)
    pieces = [here[:, start:end] for start, end in zip(LAST_CUTS, LAST_CUTS[1:])]
    arrived = [(piece, send(piece, -1), send(piece, 1)) for piece in pieces]
    token_rows = None
    for i, gathered in enumerate(map(jnp.concatenate, arrived)):
        theirs = dot32(other_choice, gathered).astype(jnp.bfloat16)
        mine = dot32(own_choice, gathered).astype(jnp.bfloat16)
        theirs = lax.ppermute(theirs, "c", SWAP)
        token_rows = place_sum(mine, theirs, LAST_CUTS[i], width, token_rows)
    return token_rows, moment_out, second_out, master_out


def solution(mesh):
    axes = ("x", "y", "z", "c")
    fine = Mesh(mesh.devices.reshape(X_SIZE, Y_SIZE, Z_SIZE, CORES), axes)
    rows = P(axes, None)
    return jax.shard_map(
        on_device,
        mesh=fine,
        in_specs=(
            rows,
            P(axes),
            P(("x", "y"), ("z", "c")),
            P(axes),
            P(axes, None, None),
            rows,
            rows,
            rows,
        ),
        out_specs=(rows, rows, rows, rows),
        check_vma=False,
    )
```
